32 devices in a mesh: dom: 32 (over z, y, x, core).
Axes of the slice: x: 2, y: 2, z: 4, core: 2. Of those that a mesh axis runs over, the one named last changes fastest.
Arguments:
- features: bfloat16 [8192, 256], P('dom'), may hold values from -48 to 48
- w_query: bfloat16 [256, 256], replicated, may hold values from -0.375 to 0.375
- w_key: bfloat16 [256, 256], replicated, may hold values from -0.375 to 0.375
- w_value: bfloat16 [256, 256], replicated, may hold values from -0.375 to 0.375
- w_out: bfloat16 [256, 256], replicated, may hold values from -0.375 to 0.375
- local_blocks: int32 [64, 4], P('dom'), may hold values from 0 to 3, as said below
- local_count: int32 [64], P('dom'), may hold values from 1 to 4, as said below
- expander_blocks: int32 [4, 64, 2], P(None, 'dom'), may hold values from 0 to 1, as said below
- expander_count: int32 [4, 64], P(None, 'dom'), may hold values from 1 to 2, as said below
Outputs:
- updated: bfloat16 [8192, 256], P('dom')
The draws below stay inside these ranges and needn't reach their ends.
Inputs may be any that keep to these rules, and one draw needn't show every extreme that they name: `local_blocks`: each row names 4 different positions of the extended range; the row of each partition's first block begins with position 0 and that of its last block with position 3. `local_count`: loads differ from partition to partition; block 0 of every partition uses its partition's largest count. `expander_blocks`: each row names 2 different blocks. `expander_count`: loads differ from partition to partition; block 0 of every partition uses its partition's largest count.
All inputs are finite; a program needn't handle non-finite values.
Results may differ from the reference program's by a relative error of at most 0.0065.
Values may be sent and summed in bfloat16 or wider, within the bound.
No kernel may reach another device: no remote copies, remote signals or barrier semaphores. Data moves between devices by JAX's collectives and lax.ppermute only.
A program may use at most 64 MiB of HBM per device.

```python
import jax
import jax.numpy as jnp
from jax import lax

D = 256
HEADS = 8
BLK = 128
NB = 2
MAXL = 4
MAXE = 2
MATCH = 4
BLOCKS = 64
NODES = 8192
N_DOM = 32


def ragged_counts(key, most):
    key_dev, key_blk = jax.random.split(key)
    device_total = BLOCKS // NB
    ceiling = jax.random.randint(key_dev, (device_total,), 1, most + 1).at[0].set(most)
    spread = jax.random.randint(key_blk, (device_total, NB), 0, 1 << 20)
    counts = 1 + spread * ceiling[:, None] // (1 << 20)
    counts = counts.at[:, 0].set(ceiling)
    return counts.reshape(BLOCKS).astype(jnp.int32)


def distinct_rows(key, row_total, choose_from, keep):
    row_keys = jax.random.split(key, row_total)
    picked = jax.vmap(lambda single: jax.random.permutation(single, choose_from)[:keep])(row_keys)
    return picked.astype(jnp.int32)


def draw_local_blocks(key, part):
    row_keys = jax.random.split(jax.random.fold_in(key, 17), BLOCKS)
    ranks = jax.vmap(lambda single: jax.random.permutation(single, NB + 2))(row_keys).astype(jnp.int32)
    within = jnp.arange(BLOCKS, dtype=jnp.int32) % NB
    position = jnp.arange(NB + 2, dtype=jnp.int32)
    first_row = (within == 0)[:, None] & (position == 0)[None, :]
    last_row = (within == NB - 1)[:, None] & (position == NB + 1)[None, :]
    ranks = jnp.where(first_row | last_row, jnp.int32(-1), ranks)
    order = jnp.argsort(ranks, axis=1, stable=True)
    return order[:, :MAXL].astype(jnp.int32)


def draw_local_count(key, part):
    return ragged_counts(jax.random.fold_in(key, 11), MAXL)


def draw_expander_blocks(key, part):
    picked = distinct_rows(jax.random.fold_in(key, 19), MATCH * BLOCKS, NB, MAXE)
    return picked.reshape(MATCH, BLOCKS, MAXE)


def draw_expander_count(key, part):
    match_keys = jax.random.split(jax.random.fold_in(key, 13), MATCH)
    return jnp.stack([ragged_counts(match_keys[m], MAXE) for m in range(MATCH)])


def draw_features(key, part):
    key_base = jax.random.fold_in(jax.random.fold_in(key, 23), 0)
    values = jnp.clip(jax.random.normal(key_base, (NODES, D), jnp.float32), -6.0, 6.0)
    return values.astype(jnp.bfloat16)


def centred(rng, shape, deviation, reach, kind=jnp.bfloat16):
    return jnp.clip(deviation * jax.random.normal(rng, shape, jnp.float32), -reach, reach).astype(kind)


def setup_inputs(seed: int = 0) -> dict:
    streams_of = jax.random.split(jax.random.key(seed), 10)
    return {
        "features": draw_features(jax.random.fold_in(streams_of[9], 71), 0),
        "w_query": centred(streams_of[1], (D, D), D ** -0.5, 0.375),
        "w_key": centred(streams_of[2], (D, D), D ** -0.5, 0.375),
        "w_value": centred(streams_of[3], (D, D), D ** -0.5, 0.375),
        "w_out": centred(streams_of[4], (D, D), D ** -0.5, 0.375),
        "local_blocks": draw_local_blocks(jax.random.fold_in(streams_of[9], 71), 0),
        "local_count": draw_local_count(jax.random.fold_in(streams_of[9], 71), 0),
        "expander_blocks": draw_expander_blocks(jax.random.fold_in(streams_of[9], 71), 0),
        "expander_count": draw_expander_count(jax.random.fold_in(streams_of[9], 71), 0),
    }


epsilon = 1e-06

def part_state(queries, kv_blocks, chosen, live_count):
    picked = kv_blocks[chosen].astype(jnp.float32)
    slot_count = chosen.shape[0]
    block_rows = kv_blocks.shape[1]
    picked = picked.reshape(slot_count * block_rows, 2, HEADS, D // HEADS)
    key_rows = picked[:, 0]
    values = picked[:, 1]
    scores = jnp.einsum('qhd,khd->hqk', queries.astype(jnp.float32), key_rows)
    usable = jnp.arange(slot_count * block_rows, dtype=jnp.int32) // block_rows < live_count
    scores = jnp.where(usable[None, None, :], scores, jnp.float32(-1e+30))
    row_max = lax.optimization_barrier(jnp.max(scores, axis=-1))
    weights = jnp.where(usable[None, None, :], jnp.exp(scores - row_max[..., None]), jnp.float32(0.0))
    weights = weights.astype(jnp.bfloat16).astype(jnp.float32)
    weight_sum = lax.optimization_barrier(jnp.sum(weights, axis=-1))
    context = jnp.einsum('hqk,khd->hqd', weights, values)
    return (row_max, weight_sum, context)

def combine(states):
    tops = jnp.stack([s[0] for s in states])
    sums = jnp.stack([s[1] for s in states])
    outs = jnp.stack([s[2] for s in states])
    highest = lax.optimization_barrier(jnp.max(tops, axis=0))
    factor = jnp.exp(tops - highest[None])
    total = lax.optimization_barrier(jnp.sum(factor * sums, axis=0))
    merged = lax.optimization_barrier(jnp.sum(factor[..., None] * outs, axis=0))
    return merged / total[..., None]

def reference(features, w_query, w_key, w_value, w_out, local_blocks, local_count, expander_blocks, expander_count):
    scaling = float(D // HEADS) ** (-0.5)
    queries = (jnp.dot(features, w_query, preferred_element_type=jnp.float32) * scaling).astype(jnp.bfloat16)
    queries = queries.reshape(N_DOM, NB, BLK, HEADS, D // HEADS)
    w_pair = jnp.concatenate([w_key, w_value], axis=1)
    pairs = jnp.dot(features, w_pair, preferred_element_type=jnp.float32).astype(jnp.bfloat16)
    pair_blocks = pairs.reshape(BLOCKS, BLK, 2 * D)
    pair_parts = pairs.reshape(N_DOM, NB, BLK, 2 * D)
    levels = N_DOM.bit_length() - 1
    node_index = jnp.arange(N_DOM, dtype=jnp.int32)
    partners = [jnp.bitwise_xor(node_index, jnp.int32(1 << m * levels // MATCH)) for m in range(MATCH)]

    def one_partition(part):
        ranged = (part * NB - 1 + jnp.arange(NB + 2, dtype=jnp.int32)) % BLOCKS
        extended = pair_blocks[ranged]
        remotes = [pair_parts[partners[m][part]] for m in range(MATCH)]

        def one_block(block):
            global_block = part * NB + block
            own_queries = queries[part, block]
            states = [part_state(own_queries, extended, local_blocks[global_block], local_count[global_block])]
            for m in range(MATCH):
                states.append(part_state(own_queries, remotes[m], expander_blocks[m, global_block], expander_count[m, global_block]))
            merged = combine(states)
            return jnp.transpose(merged, (1, 0, 2)).reshape(BLK, D).astype(jnp.bfloat16)
        return lax.map(one_block, jnp.arange(NB, dtype=jnp.int32))
    context = lax.map(one_partition, jnp.arange(N_DOM, dtype=jnp.int32)).reshape(NODES, D)
    mixed = jnp.dot(context, w_out, preferred_element_type=jnp.float32)
    normed = mixed / jnp.sqrt(lax.optimization_barrier(jnp.mean(mixed * mixed, axis=-1, keepdims=True)) + epsilon)
    return (features.astype(jnp.float32) + normed).astype(jnp.bfloat16)
```

```python
import functools

import jax
import jax.numpy as jnp
from jax import lax
from jax.experimental import pallas as pl
from jax.experimental.pallas import tpu as pltpu
from jax.sharding import PartitionSpec as P

HEADS = 8
EPSILON = 1e-06
LOW = -1e30
HIGH = 1e30

VMEM = pl.BlockSpec(memory_space=pltpu.VMEM)
SMEM = pl.BlockSpec(memory_space=pltpu.SMEM)


def matmul(a, b):
    return jnp.dot(a, b, preferred_element_type=jnp.float32)


def matmul_nt(a, b):
    return lax.dot_general(a, b, (((1,), (1,)), ((), ())), preferred_element_type=jnp.float32)


def head_of(queries_t, head):
    rows, columns = queries_t.shape
    size = rows // HEADS
    parts = []
    if head:
        parts.append(jnp.zeros((head * size, columns), queries_t.dtype))
    parts.append(queries_t[head * size : (head + 1) * size])
    if head < HEADS - 1:
        parts.append(jnp.zeros(((HEADS - 1 - head) * size, columns), queries_t.dtype))
    return jnp.concatenate(parts, axis=0)


def lanes_of_blocks(values, block_rows):
    return jnp.concatenate([jnp.full((1, block_rows), v, jnp.float32) for v in values], axis=1)


def key_value(features, w_key, w_value_t):
    keys = matmul(features, w_key).astype(jnp.bfloat16)
    values_t = matmul_nt(w_value_t, features).astype(jnp.bfloat16)
    return keys, values_t


def part_states(queries_t, parts, block_rows):
    size = queries_t.shape[0] // HEADS
    states = []
    for head in range(HEADS):
        own = head_of(queries_t, head)
        scores = []
        top = None
        for keys, values_t, uses in parts:
            part_scores = matmul(keys, own)
            for b, use in enumerate(uses):
                block = part_scores[b * block_rows : (b + 1) * block_rows]
                scores.append((block, use))
                block_top = jnp.where(use > 0, jnp.max(block, axis=0, keepdims=True), LOW)
                top = block_top if top is None else jnp.maximum(top, block_top)
        i = 0
        out = None
        for keys, values_t, uses in parts:
            weights = []
            for use in uses:
                block, use = scores[i]
                i += 1
                shift = jnp.where(use > 0, top, HIGH)
                weights.append((jnp.exp(block - shift) * use).astype(jnp.bfloat16))
            weights = jnp.concatenate(weights, axis=0)
            left = jnp.concatenate(
                [values_t[head * size : (head + 1) * size], jnp.ones((16, values_t.shape[1]), jnp.bfloat16)], axis=0
            )
            term = matmul(left, weights)
            out = term if out is None else out + term
        states.append((top, out[size : size + 1], out[:size]))
    return states


def uses_of(blocks_ref, count_ref, position, group_count, most, block_rows, lead=()):
    values = []
    for g in range(group_count):
        total = jnp.int32(0)
        for j in range(most):
            hit = (blocks_ref[(*lead, g, j)] == position) & (j < count_ref[(*lead, g)])
            total = total + hit.astype(jnp.int32)
        values.append(total.astype(jnp.float32))
    return lanes_of_blocks(values, block_rows)


def own_kernel(
    features, w_query, w_key, w_value, w_out, local_blocks, local_count,
    queries_t, w_value_t, w_out_t, tops, sums, outs,
):
    group_count, most = local_blocks.shape
    block_rows = features.shape[0] // group_count
    size = features.shape[1] // HEADS
    scaling = float(size) ** (-0.5)
    x = features[...]
    queries = (matmul(x, w_query[...]) * scaling).astype(jnp.bfloat16)
    q_t = queries.T
    v_t = w_value[...].T
    queries_t[...] = q_t
    w_value_t[...] = v_t
    w_out_t[...] = w_out[...].T
    keys, values_t = key_value(x, w_key[...], v_t)
    uses = [
        uses_of(local_blocks, local_count, 1 + b, group_count, most, block_rows)
        for b in range(group_count)
    ]
    for head, (top, total, out) in enumerate(part_states(q_t, [(keys, values_t, uses)], block_rows)):
        tops[head : head + 1] = top
        sums[head : head + 1] = total
        outs[head * size : (head + 1) * size] = out


def rest_kernel(
    features, by_core, by_1, by_2, by_3, ring,
    w_key, queries_t, w_value_t, w_out_t, tops, sums, outs,
    local_blocks, local_count, expander_blocks, expander_count, odd,
    result,
):
    group_count, most = local_blocks.shape
    most_far = expander_blocks.shape[2]
    block_rows = features.shape[0] // group_count
    size = features.shape[1] // HEADS
    w_k, v_t, q_t = w_key[...], w_value_t[...], queries_t[...]
    is_odd = odd[0]
    far = functools.partial(
        uses_of, expander_blocks, expander_count, group_count=group_count, most=most_far, block_rows=block_rows
    )
    near = functools.partial(
        uses_of, local_blocks, local_count, group_count=group_count, most=most, block_rows=block_rows
    )
    before = near(0)
    after = near(group_count + 1)
    parts = []
    for m, ref in enumerate((by_core, by_1, by_2, by_3)):
        keys, values_t = key_value(ref[...], w_k, v_t)
        uses = [far(b, lead=(m,)) for b in range(group_count)]
        if m == 0:
            uses[0] = uses[0] + jnp.where(is_odd == 0, after, 0.0)
            uses[-1] = uses[-1] + jnp.where(is_odd == 0, 0.0, before)
        parts.append((keys, values_t, uses))
    keys, values_t = key_value(ring[...], w_k, v_t)
    parts.append((keys, values_t, [jnp.where(is_odd == 0, before, after)]))
    context = []
    for head, (top, total, out) in enumerate(part_states(q_t, parts, block_rows)):
        first_top = tops[head : head + 1]
        highest = jnp.maximum(first_top, top)
        first = jnp.exp(first_top - highest)
        second = jnp.exp(top - highest)
        total = first * sums[head : head + 1] + second * total
        out = first * outs[head * size : (head + 1) * size] + second * out
        context.append((out / total).astype(jnp.bfloat16))
    context = jnp.concatenate(context, axis=0)
    mixed = matmul(w_out_t[...], context)
    normed = mixed * lax.rsqrt(jnp.mean(mixed * mixed, axis=0, keepdims=True) + EPSILON)
    result[...] = (features[...].astype(jnp.float32) + normed.T).astype(result.dtype)


def shards(
    features,
    w_query,
    w_key,
    w_value,
    w_out,
    local_blocks,
    local_count,
    expander_blocks,
    expander_count,
):
    rows, width = features.shape
    group_count = local_blocks.shape[0]
    block_rows = rows // group_count
    peers = lax.axis_size("dom")
    levels = peers.bit_length() - 1
    match_total = expander_blocks.shape[0]
    odd = lax.axis_index("dom") % 2
    arrived = []
    for matching in range(match_total):
        apart = 1 << (matching * levels // match_total)
        arrived.append(lax.ppermute(features, "dom", [(i, i ^ apart) for i in range(peers)]))
    edge = lax.dynamic_slice_in_dim(features, odd * (rows - block_rows), block_rows, axis=0)
    ring = lax.ppermute(
        edge, "dom", [(i, (i + 1) % peers if i % 2 else (i - 1) % peers) for i in range(peers)]
    )
    wide = jax.ShapeDtypeStruct((width, width), jnp.bfloat16)
    rows8 = jax.ShapeDtypeStruct((HEADS, rows), jnp.float32)
    queries_t, w_value_t, w_out_t, tops, sums, outs = pl.pallas_call(
        own_kernel,
        out_shape=(
            jax.ShapeDtypeStruct((width, rows), jnp.bfloat16),
            wide,
            wide,
            rows8,
            rows8,
            jax.ShapeDtypeStruct((width, rows), jnp.float32),
        ),
        in_specs=[VMEM] * 5 + [SMEM] * 2,
        out_specs=(VMEM,) * 6,
        compiler_params=pltpu.CompilerParams(vmem_limit_bytes=32 * 2**20),
        name="own",
    )(features, w_query, w_key, w_value, w_out, local_blocks, local_count)
    return pl.pallas_call(
        rest_kernel,
        out_shape=jax.ShapeDtypeStruct((rows, width), features.dtype),
        in_specs=[VMEM] * 13 + [SMEM] * 5,
        out_specs=VMEM,
        compiler_params=pltpu.CompilerParams(vmem_limit_bytes=32 * 2**20),
        name="rest",
    )(
        features, *arrived, ring, w_key, queries_t, w_value_t, w_out_t, tops, sums, outs,
        local_blocks, local_count, expander_blocks, expander_count, odd.reshape(1),
    )


def solution(mesh):
    in_specs = (
        P("dom", None),
        P(),
        P(),
        P(),
        P(),
        P("dom", None),
        P("dom"),
        P(None, "dom", None),
        P(None, "dom"),
    )
    out_specs = P("dom", None)
    return jax.shard_map(shards, mesh=mesh, in_specs=in_specs, out_specs=out_specs, check_vma=False)
```

```python
import jax
import jax.numpy as jnp
from jax import lax
from jax.experimental import pallas as pl
from jax.experimental.pallas import tpu as pltpu
from jax.sharding import PartitionSpec as P

HEADS = 8
EPSILON = 1e-06
LOW = -1e30

VMEM = pl.BlockSpec(memory_space=pltpu.VMEM)
ANY = pl.BlockSpec(memory_space=pl.ANY)

ORDER = tuple(range(0, HEADS, 2)) + tuple(range(1, HEADS, 2))


def matmul(a, b):
    return jnp.dot(a, b, preferred_element_type=jnp.float32)


def matmul_nt(a, b):
    return lax.dot_general(a, b, (((1,), (1,)), ((), ())), preferred_element_type=jnp.float32)


def lane_heads(width):
    return lax.broadcasted_iota(jnp.int32, (1, width), 1) // (width // HEADS)


def used(blocks, count, position, most):
    total = jnp.int32(0)
    for j in range(most):
        total = total + ((blocks(j) == position) & (j < count)).astype(jnp.int32)
    return total


def along_keys(values, block_rows):
    return jnp.concatenate([jnp.full((1, block_rows), v, jnp.float32) for v in values], axis=1)


def attend(queries, parts, groups):
    rows, width = queries.shape
    heads = lane_heads(width)
    zero = jnp.zeros((), queries.dtype)
    one = jnp.ones((), queries.dtype)
    masked = jnp.concatenate([jnp.where(heads == h, queries, zero) for h in ORDER], axis=0)

    def by_group(array):
        return array.reshape(HEADS, groups, rows // groups, array.shape[-1])

    scores = []
    top = None
    for keys, _, bias, _ in parts:
        part = by_group(matmul_nt(masked, keys)) + bias[None, :, None, :]
        part = part.reshape(HEADS * rows, keys.shape[0])
        scores.append(part)
        part_top = jnp.max(part, axis=1, keepdims=True)
        top = part_top if top is None else jnp.maximum(top, part_top)
    half = HEADS * rows // 2
    first = second = None
    for part, (keys, values, _, times) in zip(scores, parts):
        weights = jnp.exp(part - top)
        if times is not None:
            weights = (by_group(weights) * times[None, :, None, :]).reshape(HEADS * rows, keys.shape[0])
        weights = weights.astype(jnp.bfloat16)
        even = matmul(weights[:half], jnp.where(heads % 2 == 0, values, one))
        odd = matmul(weights[half:], jnp.where(heads % 2 == 1, values, one))
        first = even if first is None else first + even
        second = odd if second is None else second + odd
    tops = out = sums = jnp.zeros((rows, width), jnp.float32)
    for i, h in enumerate(ORDER):
        source, at = (first, i) if i < HEADS // 2 else (second, i - HEADS // 2)
        block = source[at * rows : (at + 1) * rows]
        out = jnp.where(heads == h, block, out)
        sums = jnp.where(heads == (h ^ 1), block, sums)
        tops = jnp.where(heads == h, top[i * rows : (i + 1) * rows], tops)
    size = width // HEADS
    sums = jnp.where(heads % 2 == 0, pltpu.roll(sums, width - size, axis=1), pltpu.roll(sums, size, axis=1))
    return tops, out, sums


def merge(one, other):
    top = jnp.maximum(one[0], other[0])
    left, right = jnp.exp(one[0] - top), jnp.exp(other[0] - top)
    return top, left * one[1] + right * other[1], left * one[2] + right * other[2]


def key_value(features, w_key, w_value):
    return matmul(features, w_key).astype(jnp.bfloat16), matmul(features, w_value).astype(jnp.bfloat16)


def own_kernel(
    features, w_query, w_key, w_value, w_out, local_blocks, local_count, expander_blocks, expander_count,
    x, key_copy, value_copy, out_copy, queries, bias, times, tops, outs, sums,
    query_copy, blocks, count, far_blocks, far_count, sems,
):
    pairs = (
        (features, x), (w_query, query_copy), (w_key, key_copy), (w_value, value_copy), (local_blocks, blocks),
        (local_count, count), (expander_blocks, far_blocks), (expander_count, far_count), (w_out, out_copy),
    )
    copies = [pltpu.make_async_copy(a, b, sems.at[i]) for i, (a, b) in enumerate(pairs)]
    for copy in copies:
        copy.start()
    groups, most = blocks.shape
    most_far, matchings = far_blocks.shape[1:]
    block_rows = x.shape[0] // groups
    size = x.shape[1] // HEADS
    is_odd = lax.rem(lax.axis_index("dom"), 2) == 1
    for copy in copies[4:8]:
        copy.wait()
    for g in range(groups):
        near = [used(lambda j: blocks[g, j], count[g], position, most) for position in range(groups + 2)]
        takes = [near[1:-1]]
        for m in range(matchings):
            takes.append(
                [used(lambda j: far_blocks[g, j, m], far_count[g, m], b, most_far) for b in range(groups)]
            )
        takes[1][0] = takes[1][0] + jnp.where(is_odd, 0, near[-1])
        takes[1][-1] = takes[1][-1] + jnp.where(is_odd, near[0], 0)
        takes.append([jnp.where(is_odd, near[-1], near[0])] * groups)
        for p, take in enumerate(takes):
            bias[p, g : g + 1, :] = along_keys([jnp.where(t > 0, 0.0, LOW) for t in take], block_rows)
        times[g : g + 1, :] = along_keys([t.astype(jnp.float32) for t in takes[1]], block_rows)
    for copy in copies[:4]:
        copy.wait()
    own = x[...]
    q = (matmul(own, query_copy[...]) * (float(size) ** -0.5)).astype(jnp.bfloat16)
    queries[...] = q
    keys, values = key_value(own, key_copy[...], value_copy[...])
    tops[...], outs[...], sums[...] = attend(q, [(keys, values, bias[0], None)], groups)
    copies[8].wait()


def middle_kernel(
    by_core, by_1, by_2, w_key, w_value, queries, bias, times, tops, outs, sums,
    new_tops, new_outs, new_sums,
):
    groups = times.shape[0]
    parts = []
    for m, ref in enumerate((by_core, by_1, by_2)):
        keys, values = key_value(ref[...], w_key[...], w_value[...])
        parts.append((keys, values, bias[1 + m], times[...] if m == 0 else None))
    state = attend(queries[...], parts, groups)
    new_tops[...], new_outs[...], new_sums[...] = merge((tops[...], outs[...], sums[...]), state)


def last_kernel(
    features, by_3, ring, w_key, w_value, w_out, queries, bias, tops, outs, sums,
    result,
):
    groups = bias.shape[1]
    block_rows = features.shape[0] // groups
    odd = lax.rem(lax.axis_index("dom"), 2)
    keys, values = key_value(by_3[...], w_key[...], w_value[...])
    parts = [(keys, values, bias[4], None)]
    edge = ring[pl.ds(pl.multiple_of((1 - odd) * ((groups - 1) * block_rows), block_rows), block_rows), :]
    keys, values = key_value(edge, w_key[...], w_value[...])
    parts.append((keys, values, bias[5][:, :block_rows], None))
    _, out, total = merge((tops[...], outs[...], sums[...]), attend(queries[...], parts, groups))
    context = (out / total).astype(jnp.bfloat16)
    mixed = matmul(context, w_out[...])
    normed = mixed * lax.rsqrt(jnp.mean(mixed * mixed, axis=1, keepdims=True) + EPSILON)
    result[...] = (features[...].astype(jnp.float32) + normed).astype(result.dtype)


def shards(
    features,
    w_query,
    w_key,
    w_value,
    w_out,
    local_blocks,
    local_count,
    expander_blocks,
    expander_count,
):
    rows, width = features.shape
    peers = lax.axis_size("dom")
    levels = peers.bit_length() - 1
    match_total = expander_blocks.shape[0]
    arrived = []
    for matching in range(match_total):
        apart = 1 << (matching * levels // match_total)
        arrived.append(lax.ppermute(features, "dom", [(i, i ^ apart) for i in range(peers)]))
    by_core, by_1, by_2, by_3 = arrived
    ring = lax.ppermute(
        features, "dom", [(i, (i + 1) % peers if i % 2 else (i - 1) % peers) for i in range(peers)]
    )
    params = pltpu.CompilerParams(vmem_limit_bytes=48 * 2**20)
    groups = local_blocks.shape[0]
    wide = jax.ShapeDtypeStruct((width, width), jnp.bfloat16)
    small = jax.ShapeDtypeStruct((rows, width), jnp.bfloat16)
    state = jax.ShapeDtypeStruct((rows, width), jnp.float32)
    far_blocks, far_count = jnp.transpose(expander_blocks, (1, 2, 0)), jnp.transpose(expander_count)
    tables = (local_blocks, local_count, far_blocks, far_count)
    inputs = (features, w_query, w_key, w_value, w_out, *tables)
    x, w_key, w_value, w_out, queries, bias, times, *states = pl.pallas_call(
        own_kernel,
        out_shape=(
            small, wide, wide, wide, small,
            jax.ShapeDtypeStruct((match_total + 2, groups, rows), jnp.float32),
            jax.ShapeDtypeStruct((groups, rows), jnp.float32),
            state, state, state,
        ),
        in_specs=[ANY] * len(inputs),
        out_specs=(VMEM,) * 10,
        scratch_shapes=[
            pltpu.VMEM((width, width), jnp.bfloat16),
            *(pltpu.SMEM(t.shape, jnp.int32) for t in tables),
            pltpu.SemaphoreType.DMA((len(inputs),)),
        ],
        compiler_params=params,
        name="own",
    )(*(pltpu.with_memory_space_constraint(a, pltpu.HBM) for a in inputs))
    states = pl.pallas_call(
        middle_kernel,
        out_shape=(state,) * 3,
        in_specs=[VMEM] * 11,
        out_specs=(VMEM,) * 3,
        compiler_params=params,
        name="middle",
    )(by_core, by_1, by_2, w_key, w_value, queries, bias, times, *states)
    return pl.pallas_call(
        last_kernel,
        out_shape=jax.ShapeDtypeStruct((rows, width), features.dtype),
        in_specs=[VMEM] * 11,
        out_specs=VMEM,
        compiler_params=params,
        name="last",
    )(x, by_3, ring, w_key, w_value, w_out, queries, bias, *states)


def solution(mesh):
    in_specs = (
        P("dom", None),
        P(),
        P(),
        P(),
        P(),
        P("dom", None),
        P("dom"),
        P(None, "dom", None),
        P(None, "dom"),
    )
    out_specs = P("dom", None)
    return jax.shard_map(shards, mesh=mesh, in_specs=in_specs, out_specs=out_specs, check_vma=False)
```

```python
import jax
import jax.numpy as jnp
from jax import lax
from jax.experimental import pallas as pl
from jax.experimental.pallas import tpu as pltpu
from jax.sharding import PartitionSpec as P

HEADS = 8
EPSILON = 1e-06
LOW = -1e30

VMEM = pl.BlockSpec(memory_space=pltpu.VMEM)
ANY = pl.BlockSpec(memory_space=pl.ANY)

ORDER = tuple(range(0, HEADS, 2)) + tuple(range(1, HEADS, 2))


def matmul(a, b):
    return jnp.dot(a, b, preferred_element_type=jnp.float32)


def matmul_nt(a, b):
    return lax.dot_general(a, b, (((1,), (1,)), ((), ())), preferred_element_type=jnp.float32)


def lane_heads(width):
    return lax.broadcasted_iota(jnp.int32, (1, width), 1) // (width // HEADS)


def used(blocks, count, position, most):
    total = jnp.int32(0)
    for j in range(most):
        total = total + ((blocks(j) == position) & (j < count)).astype(jnp.int32)
    return total


def along_keys(values, block_rows):
    return jnp.concatenate([jnp.full((1, block_rows), v, jnp.float32) for v in values], axis=1)


def attend(queries, parts, groups):
    rows, width = queries.shape
    heads = lane_heads(width)
    zero = jnp.zeros((), queries.dtype)
    one = jnp.ones((), queries.dtype)
    masked = jnp.concatenate([jnp.where(heads == h, queries, zero) for h in ORDER], axis=0)

    def by_group(array):
        return array.reshape(HEADS, groups, rows // groups, array.shape[-1])

    scores = []
    top = None
    for keys, _, bias, _ in parts:
        part = by_group(matmul_nt(masked, keys())) + bias()[None, :, None, :]
        part = part.reshape(HEADS * rows, part.shape[-1])
        scores.append(part)
        part_top = jnp.max(part, axis=1, keepdims=True)
        top = part_top if top is None else jnp.maximum(top, part_top)
    half = HEADS * rows // 2
    first = second = None
    for part, (_, values, _, times) in zip(scores, parts):
        weights = jnp.exp(part - top)
        if times is not None:
            weights = (by_group(weights) * times()[None, :, None, :]).reshape(part.shape)
        weights = weights.astype(jnp.bfloat16)
        even = matmul(weights[:half], jnp.where(heads % 2 == 0, values(), one))
        odd = matmul(weights[half:], jnp.where(heads % 2 == 1, values(), one))
        first = even if first is None else first + even
        second = odd if second is None else second + odd
    tops = out = sums = jnp.zeros((rows, width), jnp.float32)
    for i, h in enumerate(ORDER):
        source, at = (first, i) if i < HEADS // 2 else (second, i - HEADS // 2)
        block = source[at * rows : (at + 1) * rows]
        out = jnp.where(heads == h, block, out)
        sums = jnp.where(heads == (h ^ 1), block, sums)
        tops = jnp.where(heads == h, top[i * rows : (i + 1) * rows], tops)
    size = width // HEADS
    sums = jnp.where(heads % 2 == 0, pltpu.roll(sums, width - size, axis=1), pltpu.roll(sums, size, axis=1))
    return tops, out, sums


def merge(one, other):
    top = jnp.maximum(one[0], other[0])
    left, right = jnp.exp(one[0] - top), jnp.exp(other[0] - top)
    return top, left * one[1] + right * other[1], left * one[2] + right * other[2]


def project(features, w_key, w_value, keys, values, start):
    rows = pl.ds(start, features.shape[0])
    keys[rows, :] = matmul(features, w_key[...]).astype(keys.dtype)
    values[rows, :] = matmul(features, w_value[...]).astype(values.dtype)


def part_at(keys, values, start, rows, bias, times=None):
    where = pl.ds(start, rows)
    return lambda: keys[where, :], lambda: values[where, :], bias, times


def own_kernel(
    features, w_query, w_key, w_value, w_out, local_blocks, local_count, expander_blocks, expander_count,
    x, key_copy, value_copy, out_copy, queries, bias, times, tops, outs, sums,
    query_copy, keys, values, blocks, count, far_blocks, far_count, sems,
):
    pairs = (
        (features, x), (w_query, query_copy), (w_key, key_copy), (w_value, value_copy), (local_blocks, blocks),
        (local_count, count), (expander_blocks, far_blocks), (expander_count, far_count), (w_out, out_copy),
    )
    copies = [pltpu.make_async_copy(a, b, sems.at[i]) for i, (a, b) in enumerate(pairs)]
    for copy in copies:
        copy.start()
    groups, most = blocks.shape
    most_far, matchings = far_blocks.shape[1:]
    block_rows = x.shape[0] // groups
    size = x.shape[1] // HEADS
    is_odd = lax.rem(lax.axis_index("dom"), 2) == 1
    for copy in copies[4:8]:
        copy.wait()
    for g in range(groups):
        near = [used(lambda j: blocks[g, j], count[g], position, most) for position in range(groups + 2)]
        takes = [near[1:-1]]
        for m in range(matchings):
            takes.append(
                [used(lambda j: far_blocks[g, j, m], far_count[g, m], b, most_far) for b in range(groups)]
            )
        takes[1][0] = takes[1][0] + jnp.where(is_odd, 0, near[-1])
        takes[1][-1] = takes[1][-1] + jnp.where(is_odd, near[0], 0)
        takes.append([jnp.where(is_odd, near[-1], near[0])] * groups)
        for p, take in enumerate(takes):
            bias[p, g : g + 1, :] = along_keys([jnp.where(t > 0, 0.0, LOW) for t in take], block_rows)
        times[g : g + 1, :] = along_keys([t.astype(jnp.float32) for t in takes[1]], block_rows)
    for copy in copies[:4]:
        copy.wait()
    own = x[...]
    q = (matmul(own, query_copy[...]) * (float(size) ** -0.5)).astype(jnp.bfloat16)
    queries[...] = q
    project(own, key_copy, value_copy, keys, values, 0)
    parts = [part_at(keys, values, 0, own.shape[0], lambda: bias[0])]
    tops[...], outs[...], sums[...] = attend(q, parts, groups)
    copies[8].wait()


def middle_kernel(
    by_core, by_1, by_2, w_key, w_value, queries, bias, times, tops, outs, sums,
    new_tops, new_outs, new_sums,
    keys, values,
):
    groups = times.shape[0]
    rows = by_core.shape[0]
    parts = []
    for m, ref in enumerate((by_core, by_1, by_2)):
        project(ref[...], w_key, w_value, keys, values, m * rows)
        parts.append(
            part_at(keys, values, m * rows, rows, lambda m=m: bias[1 + m], (lambda: times[...]) if m == 0 else None)
        )
    state = attend(queries[...], parts, groups)
    new_tops[...], new_outs[...], new_sums[...] = merge((tops[...], outs[...], sums[...]), state)


def last_kernel(
    features, by_3, ring, w_key, w_value, w_out, queries, bias, tops, outs, sums,
    result,
    keys, values,
):
    groups = bias.shape[1]
    rows = features.shape[0]
    block_rows = rows // groups
    odd = lax.rem(lax.axis_index("dom"), 2)
    project(by_3[...], w_key, w_value, keys, values, 0)
    edge = ring[pl.ds(pl.multiple_of((1 - odd) * ((groups - 1) * block_rows), block_rows), block_rows), :]
    project(edge, w_key, w_value, keys, values, rows)
    parts = [
        part_at(keys, values, 0, rows, lambda: bias[4]),
        part_at(keys, values, rows, block_rows, lambda: bias[5, :, :block_rows]),
    ]
    _, out, total = merge((tops[...], outs[...], sums[...]), attend(queries[...], parts, groups))
    context = (out / total).astype(jnp.bfloat16)
    mixed = matmul(context, w_out[...])
    normed = mixed * lax.rsqrt(jnp.mean(mixed * mixed, axis=1, keepdims=True) + EPSILON)
    result[...] = (features[...].astype(jnp.float32) + normed).astype(result.dtype)


def shards(
    features,
    w_query,
    w_key,
    w_value,
    w_out,
    local_blocks,
    local_count,
    expander_blocks,
    expander_count,
):
    rows, width = features.shape
    peers = lax.axis_size("dom")
    levels = peers.bit_length() - 1
    match_total = expander_blocks.shape[0]
    arrived = []
    for matching in range(match_total):
        apart = 1 << (matching * levels // match_total)
        arrived.append(lax.ppermute(features, "dom", [(i, i ^ apart) for i in range(peers)]))
    by_core, by_1, by_2, by_3 = arrived
    ring = lax.ppermute(
        features, "dom", [(i, (i + 1) % peers if i % 2 else (i - 1) % peers) for i in range(peers)]
    )
    params = pltpu.CompilerParams(vmem_limit_bytes=48 * 2**20)
    groups = local_blocks.shape[0]
    wide = jax.ShapeDtypeStruct((width, width), jnp.bfloat16)
    small = jax.ShapeDtypeStruct((rows, width), jnp.bfloat16)
    state = jax.ShapeDtypeStruct((rows, width), jnp.float32)

    def pairs_of(total):
        return [pltpu.VMEM((total, width), jnp.bfloat16)] * 2

    far_blocks, far_count = jnp.transpose(expander_blocks, (1, 2, 0)), jnp.transpose(expander_count)
    tables = (local_blocks, local_count, far_blocks, far_count)
    inputs = (features, w_query, w_key, w_value, w_out, *tables)
    x, w_key, w_value, w_out, queries, bias, times, *states = pl.pallas_call(
        own_kernel,
        out_shape=(
            small, wide, wide, wide, small,
            jax.ShapeDtypeStruct((match_total + 2, groups, rows), jnp.float32),
            jax.ShapeDtypeStruct((groups, rows), jnp.float32),
            state, state, state,
        ),
        in_specs=[ANY] * len(inputs),
        out_specs=(VMEM,) * 10,
        scratch_shapes=[
            pltpu.VMEM((width, width), jnp.bfloat16),
            *pairs_of(rows),
            *(pltpu.SMEM(t.shape, jnp.int32) for t in tables),
            pltpu.SemaphoreType.DMA((len(inputs),)),
        ],
        compiler_params=params,
        name="own",
    )(*(pltpu.with_memory_space_constraint(a, pltpu.HBM) for a in inputs))
    states = pl.pallas_call(
        middle_kernel,
        out_shape=(state,) * 3,
        in_specs=[VMEM] * 11,
        out_specs=(VMEM,) * 3,
        scratch_shapes=pairs_of(3 * rows),
        compiler_params=params,
        name="middle",
    )(by_core, by_1, by_2, w_key, w_value, queries, bias, times, *states)
    return pl.pallas_call(
        last_kernel,
        out_shape=jax.ShapeDtypeStruct((rows, width), features.dtype),
        in_specs=[VMEM] * 11,
        out_specs=VMEM,
        scratch_shapes=pairs_of(rows + rows // groups),
        compiler_params=params,
        name="last",
    )(x, by_3, ring, w_key, w_value, w_out, queries, bias, *states)


def solution(mesh):
    in_specs = (
        P("dom", None),
        P(),
        P(),
        P(),
        P(),
        P("dom", None),
        P("dom"),
        P(None, "dom", None),
        P(None, "dom"),
    )
    out_specs = P("dom", None)
    return jax.shard_map(shards, mesh=mesh, in_specs=in_specs, out_specs=out_specs, check_vma=False)
```

```python
import jax
import jax.numpy as jnp
from jax import lax
from jax.experimental import pallas as pl
from jax.experimental.pallas import tpu as pltpu
from jax.sharding import PartitionSpec as P

HEADS = 8
EPSILON = 1e-06
LOW = -1e30

VMEM = pl.BlockSpec(memory_space=pltpu.VMEM)
ANY = pl.BlockSpec(memory_space=pl.ANY)

ORDER = tuple(range(0, HEADS, 2)) + tuple(range(1, HEADS, 2))


def matmul(a, b):
    return jnp.dot(a, b, preferred_element_type=jnp.float32)


def matmul_nt(a, b):
    return lax.dot_general(a, b, (((1,), (1,)), ((), ())), preferred_element_type=jnp.float32)


def lane_heads(width):
    return lax.broadcasted_iota(jnp.int32, (1, width), 1) // (width // HEADS)


def used(blocks, count, position, most):
    total = jnp.int32(0)
    for j in range(most):
        total = total + ((blocks(j) == position) & (j < count)).astype(jnp.int32)
    return total


def along_keys(values, block_rows):
    return jnp.concatenate([jnp.full((1, block_rows), v, jnp.float32) for v in values], axis=1)


def attend(queries, parts, groups):
    rows, width = queries.shape
    heads = lane_heads(width)
    zero = jnp.zeros((), queries.dtype)
    one = jnp.ones((), queries.dtype)
    masked = jnp.concatenate([jnp.where(heads == h, queries, zero) for h in ORDER], axis=0)

    def by_group(array):
        return array.reshape(HEADS, groups, rows // groups, array.shape[-1])

    scores = []
    top = None
    for keys, _, bias, _ in parts:
        part = by_group(matmul_nt(masked, keys())) + bias()[None, :, None, :]
        part = part.reshape(HEADS * rows, part.shape[-1])
        scores.append(part)
        part_top = jnp.max(part, axis=1, keepdims=True)
        top = part_top if top is None else jnp.maximum(top, part_top)
    half = HEADS * rows // 2
    first = second = None
    for part, (_, values, _, times) in zip(scores, parts):
        weights = jnp.exp(part - top)
        if times is not None:
            weights = (by_group(weights) * times()[None, :, None, :]).reshape(part.shape)
        weights = weights.astype(jnp.bfloat16)
        even = jnp.where(heads % 2 == 0, values(), one)
        first = matmul(weights[:half], even) if first is None else first + matmul(weights[:half], even)
        odd = jnp.where(heads % 2 == 1, values(), one)
        second = matmul(weights[half:], odd) if second is None else second + matmul(weights[half:], odd)
    tops = out = sums = jnp.zeros((rows, width), jnp.float32)
    for i, h in enumerate(ORDER):
        source, at = (first, i) if i < HEADS // 2 else (second, i - HEADS // 2)
        block = source[at * rows : (at + 1) * rows]
        out = jnp.where(heads == h, block, out)
        sums = jnp.where(heads == (h ^ 1), block, sums)
        tops = jnp.where(heads == h, top[i * rows : (i + 1) * rows], tops)
    size = width // HEADS
    sums = jnp.where(heads % 2 == 0, pltpu.roll(sums, width - size, axis=1), pltpu.roll(sums, size, axis=1))
    return tops, out, sums


def merge(one, other):
    top = jnp.maximum(one[0], other[0])
    left, right = jnp.exp(one[0] - top), jnp.exp(other[0] - top)
    return top, left * one[1] + right * other[1], left * one[2] + right * other[2]


def project(features, w_key, w_value, keys, values, start):
    rows = pl.ds(start, features.shape[0])
    keys[rows, :] = matmul(features, w_key[...]).astype(keys.dtype)
    values[rows, :] = matmul(features, w_value[...]).astype(values.dtype)


def part_at(keys, values, start, rows, bias, times=None):
    where = pl.ds(start, rows)
    return lambda: keys[where, :], lambda: values[where, :], bias, times


def own_kernel(
    features, w_query, w_key, w_value, w_out, local_blocks, local_count, expander_blocks, expander_count,
    x, key_copy, value_copy, out_copy, queries, bias, times, tops, outs, sums,
    query_copy, keys, values, blocks, count, far_blocks, far_count, sems,
):
    pairs = (
        (features, x), (w_query, query_copy), (w_key, key_copy), (w_value, value_copy), (local_blocks, blocks),
        (local_count, count), (expander_blocks, far_blocks), (expander_count, far_count), (w_out, out_copy),
    )
    copies = [pltpu.make_async_copy(a, b, sems.at[i]) for i, (a, b) in enumerate(pairs)]
    for copy in copies:
        copy.start()
    groups, most = blocks.shape
    most_far, matchings = far_blocks.shape[1:]
    block_rows = x.shape[0] // groups
    size = x.shape[1] // HEADS
    is_odd = lax.rem(lax.axis_index("dom"), 2) == 1
    for copy in copies[4:8]:
        copy.wait()
    for g in range(groups):
        near = [used(lambda j: blocks[g, j], count[g], position, most) for position in range(groups + 2)]
        takes = [near[1:-1]]
        for m in range(matchings):
            takes.append(
                [used(lambda j: far_blocks[g, j, m], far_count[g, m], b, most_far) for b in range(groups)]
            )
        takes[1][0] = takes[1][0] + jnp.where(is_odd, 0, near[-1])
        takes[1][-1] = takes[1][-1] + jnp.where(is_odd, near[0], 0)
        takes.append([jnp.where(is_odd, near[-1], near[0])] * groups)
        for p, take in enumerate(takes):
            bias[p, g : g + 1, :] = along_keys([jnp.where(t > 0, 0.0, LOW) for t in take], block_rows)
        times[g : g + 1, :] = along_keys([t.astype(jnp.float32) for t in takes[1]], block_rows)
    for copy in copies[:4]:
        copy.wait()
    own = x[...]
    q = (matmul(own, query_copy[...]) * (float(size) ** -0.5)).astype(jnp.bfloat16)
    queries[...] = q
    project(own, key_copy, value_copy, keys, values, 0)
    parts = [part_at(keys, values, 0, own.shape[0], lambda: bias[0])]
    tops[...], outs[...], sums[...] = attend(q, parts, groups)
    copies[8].wait()


def middle_kernel(
    by_core, by_1, by_2, w_key, w_value, queries, bias, times, tops, outs, sums,
    new_tops, new_outs, new_sums,
    keys, values,
):
    groups = times.shape[0]
    rows = by_core.shape[0]
    parts = []
    for m, ref in enumerate((by_core, by_1, by_2)):
        project(ref[...], w_key, w_value, keys, values, m * rows)
        parts.append(
            part_at(keys, values, m * rows, rows, lambda m=m: bias[1 + m], (lambda: times[...]) if m == 0 else None)
        )
    state = attend(queries[...], parts, groups)
    new_tops[...], new_outs[...], new_sums[...] = merge((tops[...], outs[...], sums[...]), state)


def last_kernel(
    features, by_3, ring, w_key, w_value, w_out, queries, bias, tops, outs, sums,
    result,
    keys, values,
):
    groups = bias.shape[1]
    rows = features.shape[0]
    block_rows = rows // groups
    odd = lax.rem(lax.axis_index("dom"), 2)
    project(by_3[...], w_key, w_value, keys, values, 0)
    edge = ring[pl.ds(pl.multiple_of((1 - odd) * ((groups - 1) * block_rows), block_rows), block_rows), :]
    project(edge, w_key, w_value, keys, values, rows)
    parts = [
        part_at(keys, values, 0, rows, lambda: bias[4]),
        part_at(keys, values, rows, block_rows, lambda: bias[5, :, :block_rows]),
    ]
    _, out, total = merge((tops[...], outs[...], sums[...]), attend(queries[...], parts, groups))
    context = (out / total).astype(jnp.bfloat16)
    mixed = matmul(context, w_out[...])
    normed = mixed * lax.rsqrt(jnp.mean(mixed * mixed, axis=1, keepdims=True) + EPSILON)
    result[...] = (features[...].astype(jnp.float32) + normed).astype(result.dtype)


def shards(
    features,
    w_query,
    w_key,
    w_value,
    w_out,
    local_blocks,
    local_count,
    expander_blocks,
    expander_count,
):
    rows, width = features.shape
    peers = lax.axis_size("dom")
    levels = peers.bit_length() - 1
    match_total = expander_blocks.shape[0]
    arrived = []
    for matching in range(match_total):
        apart = 1 << (matching * levels // match_total)
        arrived.append(lax.ppermute(features, "dom", [(i, i ^ apart) for i in range(peers)]))
    by_core, by_1, by_2, by_3 = arrived
    ring = lax.ppermute(
        features, "dom", [(i, (i + 1) % peers if i % 2 else (i - 1) % peers) for i in range(peers)]
    )
    params = pltpu.CompilerParams(vmem_limit_bytes=48 * 2**20)
    groups = local_blocks.shape[0]
    wide = jax.ShapeDtypeStruct((width, width), jnp.bfloat16)
    small = jax.ShapeDtypeStruct((rows, width), jnp.bfloat16)
    state = jax.ShapeDtypeStruct((rows, width), jnp.float32)

    def pairs_of(total):
        return [pltpu.VMEM((total, width), jnp.bfloat16)] * 2

    far_blocks, far_count = jnp.transpose(expander_blocks, (1, 2, 0)), jnp.transpose(expander_count)
    tables = (local_blocks, local_count, far_blocks, far_count)
    inputs = (features, w_query, w_key, w_value, w_out, *tables)
    x, w_key, w_value, w_out, queries, bias, times, *states = pl.pallas_call(
        own_kernel,
        out_shape=(
            small, wide, wide, wide, small,
            jax.ShapeDtypeStruct((match_total + 2, groups, rows), jnp.float32),
            jax.ShapeDtypeStruct((groups, rows), jnp.float32),
            state, state, state,
        ),
        in_specs=[ANY] * len(inputs),
        out_specs=(VMEM,) * 10,
        scratch_shapes=[
            pltpu.VMEM((width, width), jnp.bfloat16),
            *pairs_of(rows),
            *(pltpu.SMEM(t.shape, jnp.int32) for t in tables),
            pltpu.SemaphoreType.DMA((len(inputs),)),
        ],
        compiler_params=params,
        name="own",
    )(*(pltpu.with_memory_space_constraint(a, pltpu.HBM) for a in inputs))
    states = pl.pallas_call(
        middle_kernel,
        out_shape=(state,) * 3,
        in_specs=[VMEM] * 11,
        out_specs=(VMEM,) * 3,
        scratch_shapes=pairs_of(3 * rows),
        compiler_params=params,
        name="middle",
    )(by_core, by_1, by_2, w_key, w_value, queries, bias, times, *states)
    return pl.pallas_call(
        last_kernel,
        out_shape=jax.ShapeDtypeStruct((rows, width), features.dtype),
        in_specs=[VMEM] * 11,
        out_specs=VMEM,
        scratch_shapes=pairs_of(rows + rows // groups),
        compiler_params=params,
        name="last",
    )(x, by_3, ring, w_key, w_value, w_out, queries, bias, *states)


def solution(mesh):
    in_specs = (
        P("dom", None),
        P(),
        P(),
        P(),
        P(),
        P("dom", None),
        P("dom"),
        P(None, "dom", None),
        P(None, "dom"),
    )
    out_specs = P("dom", None)
    return jax.shard_map(shards, mesh=mesh, in_specs=in_specs, out_specs=out_specs, check_vma=False)
```

```python
import jax
import jax.numpy as jnp
from jax import lax
from jax.experimental import pallas as pl
from jax.experimental.pallas import tpu as pltpu
from jax.sharding import PartitionSpec as P

HEADS = 8
EPSILON = 1e-06
LOW = -1e30

VMEM = pl.BlockSpec(memory_space=pltpu.VMEM)
ANY = pl.BlockSpec(memory_space=pl.ANY)

ORDER = tuple(range(0, HEADS, 2)) + tuple(range(1, HEADS, 2))


def matmul(a, b):
    return jnp.dot(a, b, preferred_element_type=jnp.float32)


def matmul_nt(a, b):
    return lax.dot_general(a, b, (((1,), (1,)), ((), ())), preferred_element_type=jnp.float32)


def lane_heads(width):
    return lax.broadcasted_iota(jnp.int32, (1, width), 1) // (width // HEADS)


def used(blocks, count, position, most):
    total = jnp.int32(0)
    for j in range(most):
        total = total + ((blocks(j) == position) & (j < count)).astype(jnp.int32)
    return total


def along_keys(values, block_rows):
    return jnp.concatenate([jnp.full((1, block_rows), v, jnp.float32) for v in values], axis=1)


def attend(queries, parts, groups):
    rows, width = queries.shape
    heads = lane_heads(width)
    zero = jnp.zeros((), queries.dtype)
    one = jnp.ones((), queries.dtype)
    masked = jnp.concatenate([jnp.where(heads == h, queries, zero) for h in ORDER], axis=0)

    def by_group(array):
        return array.reshape(HEADS, groups, rows // groups, array.shape[-1])

    scores = []
    top = None
    for keys, _, bias, _ in parts:
        part = by_group(matmul_nt(masked, keys())) + bias()[None, :, None, :]
        part = part.reshape(HEADS * rows, part.shape[-1])
        scores.append(part)
        part_top = jnp.max(part, axis=1, keepdims=True)
        top = part_top if top is None else jnp.maximum(top, part_top)
    half = HEADS * rows // 2
    first = second = None
    for part, (_, values, _, times) in zip(scores, parts):
        weights = jnp.exp(part - top)
        if times is not None:
            weights = (by_group(weights) * times()[None, :, None, :]).reshape(part.shape)
        weights = weights.astype(jnp.bfloat16)
        even = jnp.where(heads % 2 == 0, values(), one)
        first = matmul(weights[:half], even) if first is None else first + matmul(weights[:half], even)
        odd = jnp.where(heads % 2 == 1, values(), one)
        second = matmul(weights[half:], odd) if second is None else second + matmul(weights[half:], odd)
    tops = out = sums = jnp.zeros((rows, width), jnp.float32)
    for i, h in enumerate(ORDER):
        source, at = (first, i) if i < HEADS // 2 else (second, i - HEADS // 2)
        block = source[at * rows : (at + 1) * rows]
        out = jnp.where(heads == h, block, out)
        sums = jnp.where(heads == (h ^ 1), block, sums)
        tops = jnp.where(heads == h, top[i * rows : (i + 1) * rows], tops)
    size = width // HEADS
    sums = jnp.where(heads % 2 == 0, pltpu.roll(sums, width - size, axis=1), pltpu.roll(sums, size, axis=1))
    return tops, out, sums


def merge(one, other):
    top = jnp.maximum(one[0], other[0])
    left, right = jnp.exp(one[0] - top), jnp.exp(other[0] - top)
    return top, left * one[1] + right * other[1], left * one[2] + right * other[2]


def project(features, w_key, w_value, keys, values, start):
    rows = pl.ds(start, features.shape[0])
    keys[rows, :] = matmul(features, w_key[...]).astype(keys.dtype)
    values[rows, :] = matmul(features, w_value[...]).astype(values.dtype)


def part_at(keys, values, start, rows, bias, times=None):
    where = pl.ds(start, rows)
    return lambda: keys[where, :], lambda: values[where, :], bias, times


def load_kernel(
    features, w_query, w_key, w_value, w_out, local_blocks, local_count, expander_blocks, expander_count,
    x, key_copy, value_copy, out_copy, queries, keys, values, bias, times, trailing, leading,
    query_copy, blocks, count, far_blocks, far_count, sems,
):
    pairs = (
        (features, x), (w_query, query_copy), (w_key, key_copy), (w_value, value_copy), (local_blocks, blocks),
        (local_count, count), (expander_blocks, far_blocks), (expander_count, far_count), (w_out, out_copy),
    )
    copies = [pltpu.make_async_copy(a, b, sems.at[i]) for i, (a, b) in enumerate(pairs)]
    for copy in copies:
        copy.start()
    groups, most = blocks.shape
    most_far, matchings = far_blocks.shape[1:]
    rows, width = x.shape
    block_rows = rows // groups
    size = width // HEADS
    is_odd = lax.rem(lax.axis_index("dom"), 2) == 1
    for copy in copies[4:8]:
        copy.wait()
    for g in range(groups):
        near = [used(lambda j: blocks[g, j], count[g], position, most) for position in range(groups + 2)]
        takes = [near[1:-1]]
        for m in range(matchings):
            takes.append(
                [used(lambda j: far_blocks[g, j, m], far_count[g, m], b, most_far) for b in range(groups)]
            )
        takes[1][0] = takes[1][0] + jnp.where(is_odd, 0, near[-1])
        takes[1][-1] = takes[1][-1] + jnp.where(is_odd, near[0], 0)
        takes.append([jnp.where(is_odd, near[-1], near[0])] * groups)
        for p, take in enumerate(takes):
            bias[p, g : g + 1, :] = along_keys([jnp.where(t > 0, 0.0, LOW) for t in take], block_rows)
        times[g : g + 1, :] = along_keys([t.astype(jnp.float32) for t in takes[1]], block_rows)
    for copy in copies[:4]:
        copy.wait()
    own = x[...]
    trailing[...] = x[rows - block_rows :, :]
    leading[...] = x[:block_rows, :]
    queries[...] = (matmul(own, query_copy[...]) * (float(size) ** -0.5)).astype(jnp.bfloat16)
    project(own, key_copy, value_copy, keys, values, 0)
    copies[8].wait()


def near_kernel(
    own_keys, own_values, by_core, by_1, leading, w_key, w_value, queries, bias, times,
    tops, outs, sums, leading_copy,
    keys, values,
):
    groups = times.shape[0]
    rows = by_core.shape[0]
    leading_copy[...] = leading[...]
    project(by_core[...], w_key, w_value, keys, values, 0)
    project(by_1[...], w_key, w_value, keys, values, rows)
    parts = [
        part_at(own_keys, own_values, 0, rows, lambda: bias[0]),
        part_at(keys, values, 0, rows, lambda: bias[1], lambda: times[...]),
        part_at(keys, values, rows, rows, lambda: bias[2]),
    ]
    tops[...], outs[...], sums[...] = attend(queries[...], parts, groups)


def last_kernel(
    features, by_2, by_3, before, after, w_key, w_value, w_out, queries, bias, tops, outs, sums,
    result,
    keys, values,
):
    groups = bias.shape[1]
    rows = features.shape[0]
    block_rows = rows // groups
    is_odd = lax.rem(lax.axis_index("dom"), 2) == 1
    project(by_2[...], w_key, w_value, keys, values, 0)
    project(by_3[...], w_key, w_value, keys, values, rows)
    edge = jnp.where(is_odd, after[...], before[...])
    project(edge, w_key, w_value, keys, values, 2 * rows)
    parts = [
        part_at(keys, values, 0, rows, lambda: bias[3]),
        part_at(keys, values, rows, rows, lambda: bias[4]),
        part_at(keys, values, 2 * rows, block_rows, lambda: bias[5, :, :block_rows]),
    ]
    _, out, total = merge((tops[...], outs[...], sums[...]), attend(queries[...], parts, groups))
    context = (out / total).astype(jnp.bfloat16)
    mixed = matmul(context, w_out[...])
    normed = mixed * lax.rsqrt(jnp.mean(mixed * mixed, axis=1, keepdims=True) + EPSILON)
    result[...] = (features[...].astype(jnp.float32) + normed).astype(result.dtype)


def shards(
    features,
    w_query,
    w_key,
    w_value,
    w_out,
    local_blocks,
    local_count,
    expander_blocks,
    expander_count,
):
    rows, width = features.shape
    groups = local_blocks.shape[0]
    block_rows = rows // groups
    peers = lax.axis_size("dom")
    levels = peers.bit_length() - 1
    match_total = expander_blocks.shape[0]
    arrived = []
    for matching in range(match_total):
        apart = 1 << (matching * levels // match_total)
        arrived.append(lax.ppermute(features, "dom", [(i, i ^ apart) for i in range(peers)]))
    by_core, by_1, by_2, by_3 = arrived
    params = pltpu.CompilerParams(vmem_limit_bytes=48 * 2**20)

    def array(*shape, dtype=jnp.bfloat16):
        return jax.ShapeDtypeStruct(shape, dtype)

    def pairs_of(total):
        return [pltpu.VMEM((total, width), jnp.bfloat16)] * 2

    state = [array(rows, width, dtype=jnp.float32)] * 3
    far_blocks, far_count = jnp.transpose(expander_blocks, (1, 2, 0)), jnp.transpose(expander_count)
    tables = (local_blocks, local_count, far_blocks, far_count)
    inputs = (features, w_query, w_key, w_value, w_out, *tables)
    x, w_key, w_value, w_out, queries, own_keys, own_values, bias, times, trailing, leading = pl.pallas_call(
        load_kernel,
        out_shape=(
            array(rows, width), *[array(width, width)] * 3, *[array(rows, width)] * 3,
            array(match_total + 2, groups, rows, dtype=jnp.float32), array(groups, rows, dtype=jnp.float32),
            array(block_rows, width), array(block_rows, width),
        ),
        in_specs=[ANY] * len(inputs),
        out_specs=(VMEM,) * 11,
        scratch_shapes=[
            pltpu.VMEM((width, width), jnp.bfloat16),
            *(pltpu.SMEM(t.shape, jnp.int32) for t in tables),
            pltpu.SemaphoreType.DMA((len(inputs),)),
        ],
        compiler_params=params,
        name="load",
    )(*(pltpu.with_memory_space_constraint(a, pltpu.HBM) for a in inputs))
    before = lax.ppermute(trailing, "dom", [(i, (i + 1) % peers) for i in range(peers)])
    *states, leading = pl.pallas_call(
        near_kernel,
        out_shape=(*state, array(block_rows, width)),
        in_specs=[VMEM] * 10,
        out_specs=(VMEM,) * 4,
        scratch_shapes=pairs_of(2 * rows),
        compiler_params=params,
        name="near",
    )(own_keys, own_values, by_core, by_1, leading, w_key, w_value, queries, bias, times)
    after = lax.ppermute(leading, "dom", [(i, (i - 1) % peers) for i in range(peers)])
    return pl.pallas_call(
        last_kernel,
        out_shape=array(rows, width, dtype=features.dtype),
        in_specs=[VMEM] * 13,
        out_specs=VMEM,
        scratch_shapes=pairs_of(2 * rows + block_rows),
        compiler_params=params,
        name="last",
    )(x, by_2, by_3, before, after, w_key, w_value, w_out, queries, bias, *states)


def solution(mesh):
    in_specs = (
        P("dom", None),
        P(),
        P(),
        P(),
        P(),
        P("dom", None),
        P("dom"),
        P(None, "dom", None),
        P(None, "dom"),
    )
    out_specs = P("dom", None)
    return jax.shard_map(shards, mesh=mesh, in_specs=in_specs, out_specs=out_specs, check_vma=False)
```

```python
import jax
import jax.numpy as jnp
from jax import lax
from jax.experimental import pallas as pl
from jax.experimental.pallas import tpu as pltpu
from jax.sharding import PartitionSpec as P

HEADS = 8
EPSILON = 1e-06
LOW = -1e30

VMEM = pl.BlockSpec(memory_space=pltpu.VMEM)
ANY = pl.BlockSpec(memory_space=pl.ANY)

ORDER = tuple(range(0, HEADS, 2)) + tuple(range(1, HEADS, 2))


def matmul(a, b):
    return jnp.dot(a, b, preferred_element_type=jnp.float32)


def matmul_nt(a, b):
    return lax.dot_general(a, b, (((1,), (1,)), ((), ())), preferred_element_type=jnp.float32)


def lane_heads(width):
    return lax.broadcasted_iota(jnp.int32, (1, width), 1) // (width // HEADS)


def used(blocks, count, position, most):
    total = jnp.int32(0)
    for j in range(most):
        total = total + ((blocks(j) == position) & (j < count)).astype(jnp.int32)
    return total


def along_keys(values, block_rows):
    return jnp.concatenate([jnp.full((1, block_rows), v, jnp.float32) for v in values], axis=1)


def attend(queries, parts, groups):
    rows, width = queries.shape
    heads = lane_heads(width)
    zero = jnp.zeros((), queries.dtype)
    one = jnp.ones((), queries.dtype)
    masked = jnp.concatenate([jnp.where(heads == h, queries, zero) for h in ORDER], axis=0)

    def by_group(array):
        return array.reshape(HEADS, groups, rows // groups, array.shape[-1])

    scores = []
    top = None
    for keys, _, bias, _ in parts:
        part = by_group(matmul_nt(masked, keys())) + bias()[None, :, None, :]
        part = part.reshape(HEADS * rows, part.shape[-1])
        scores.append(part)
        part_top = jnp.max(part, axis=1, keepdims=True)
        top = part_top if top is None else jnp.maximum(top, part_top)
    half = HEADS * rows // 2
    first = second = None
    for part, (_, values, _, times) in zip(scores, parts):
        weights = jnp.exp(part - top)
        if times is not None:
            weights = (by_group(weights) * times()[None, :, None, :]).reshape(part.shape)
        weights = weights.astype(jnp.bfloat16)
        even = jnp.where(heads % 2 == 0, values(), one)
        first = matmul(weights[:half], even) if first is None else first + matmul(weights[:half], even)
        odd = jnp.where(heads % 2 == 1, values(), one)
        second = matmul(weights[half:], odd) if second is None else second + matmul(weights[half:], odd)
    tops = out = sums = jnp.zeros((rows, width), jnp.float32)
    for i, h in enumerate(ORDER):
        source, at = (first, i) if i < HEADS // 2 else (second, i - HEADS // 2)
        block = source[at * rows : (at + 1) * rows]
        out = jnp.where(heads == h, block, out)
        sums = jnp.where(heads == (h ^ 1), block, sums)
        tops = jnp.where(heads == h, top[i * rows : (i + 1) * rows], tops)
    size = width // HEADS
    sums = jnp.where(heads % 2 == 0, pltpu.roll(sums, width - size, axis=1), pltpu.roll(sums, size, axis=1))
    return tops, out, sums


def merge(one, other):
    top = jnp.maximum(one[0], other[0])
    left, right = jnp.exp(one[0] - top), jnp.exp(other[0] - top)
    return top, left * one[1] + right * other[1], left * one[2] + right * other[2]


def project(features, w_key, w_value, keys, values, start):
    rows = pl.ds(start, features.shape[0])
    keys[rows, :] = matmul(features, w_key[...]).astype(keys.dtype)
    values[rows, :] = matmul(features, w_value[...]).astype(values.dtype)


def part_at(keys, values, start, rows, bias, times=None):
    where = pl.ds(start, rows)
    return lambda: keys[where, :], lambda: values[where, :], bias, times


def own_kernel(
    features, w_query, w_key, w_value, w_out, local_blocks, local_count, expander_blocks, expander_count,
    x, key_copy, value_copy, out_copy, queries, bias, times, tops, outs, sums,
    query_copy, keys, values, blocks, count, far_blocks, far_count, sems,
):
    pairs = (
        (features, x), (w_query, query_copy), (w_key, key_copy), (w_value, value_copy), (local_blocks, blocks),
        (local_count, count), (expander_blocks, far_blocks), (expander_count, far_count), (w_out, out_copy),
    )
    copies = [pltpu.make_async_copy(a, b, sems.at[i]) for i, (a, b) in enumerate(pairs)]
    for copy in copies:
        copy.start()
    groups, most = blocks.shape
    most_far, matchings = far_blocks.shape[1:]
    rows, width = x.shape
    block_rows = rows // groups
    size = width // HEADS
    is_odd = lax.rem(lax.axis_index("dom"), 2) == 1
    for copy in copies[4:8]:
        copy.wait()
    for g in range(groups):
        near = [used(lambda j: blocks[g, j], count[g], position, most) for position in range(groups + 2)]
        takes = [near[1:-1]]
        for m in range(matchings):
            takes.append(
                [used(lambda j: far_blocks[g, j, m], far_count[g, m], b, most_far) for b in range(groups)]
            )
        takes[1][0] = takes[1][0] + jnp.where(is_odd, 0, near[-1])
        takes[1][-1] = takes[1][-1] + jnp.where(is_odd, near[0], 0)
        takes.append([jnp.where(is_odd, near[-1], near[0])] * groups)
        for p, take in enumerate(takes):
            bias[p, g : g + 1, :] = along_keys([jnp.where(t > 0, 0.0, LOW) for t in take], block_rows)
        times[g : g + 1, :] = along_keys([t.astype(jnp.float32) for t in takes[1]], block_rows)
    for copy in copies[:4]:
        copy.wait()
    own = x[...]
    q = (matmul(own, query_copy[...]) * (float(size) ** -0.5)).astype(jnp.bfloat16)
    queries[...] = q
    project(own, key_copy, value_copy, keys, values, 0)
    parts = [part_at(keys, values, 0, rows, lambda: bias[0])]
    tops[...], outs[...], sums[...] = attend(q, parts, groups)
    copies[8].wait()


def rest_kernel(
    features, before, by_1, by_2, by_3, after, w_key, w_value, w_out, queries, bias, times, tops, outs, sums,
    result,
    keys, values,
):
    groups = times.shape[0]
    rows = features.shape[0]
    block_rows = rows // groups
    is_odd = lax.rem(lax.axis_index("dom"), 2) == 1
    project(by_1[...], w_key, w_value, keys, values, 0)
    project(by_2[...], w_key, w_value, keys, values, rows)
    project(by_3[...], w_key, w_value, keys, values, 2 * rows)
    project(jnp.where(is_odd, before[...], after[...]), w_key, w_value, keys, values, 3 * rows)
    edge = jnp.where(is_odd, after[:block_rows, :], before[rows - block_rows :, :])
    project(edge, w_key, w_value, keys, values, 4 * rows)
    parts = [part_at(keys, values, m * rows, rows, lambda m=m: bias[2 + m]) for m in range(3)]
    parts.append(part_at(keys, values, 3 * rows, rows, lambda: bias[1], lambda: times[...]))
    parts.append(part_at(keys, values, 4 * rows, block_rows, lambda: bias[5, :, :block_rows]))
    _, out, total = merge((tops[...], outs[...], sums[...]), attend(queries[...], parts, groups))
    context = (out / total).astype(jnp.bfloat16)
    mixed = matmul(context, w_out[...])
    normed = mixed * lax.rsqrt(jnp.mean(mixed * mixed, axis=1, keepdims=True) + EPSILON)
    result[...] = (features[...].astype(jnp.float32) + normed).astype(result.dtype)


def shards(
    features,
    w_query,
    w_key,
    w_value,
    w_out,
    local_blocks,
    local_count,
    expander_blocks,
    expander_count,
):
    rows, width = features.shape
    groups = local_blocks.shape[0]
    block_rows = rows // groups
    peers = lax.axis_size("dom")
    levels = peers.bit_length() - 1
    match_total = expander_blocks.shape[0]
    params = pltpu.CompilerParams(vmem_limit_bytes=48 * 2**20)

    def array(*shape, dtype=jnp.bfloat16):
        return jax.ShapeDtypeStruct(shape, dtype)

    def pairs_of(total):
        return [pltpu.VMEM((total, width), jnp.bfloat16)] * 2

    def exchange(matching):
        apart = 1 << (matching * levels // match_total)
        return lax.ppermute(features, "dom", [(i, i ^ apart) for i in range(peers)])

    before = lax.ppermute(features, "dom", [(i, (i + 1) % peers) for i in range(peers)])
    by_1, by_2, by_3 = (exchange(m) for m in range(1, match_total))
    after = lax.ppermute(features, "dom", [(i, (i - 1) % peers) for i in range(peers)])
    far_blocks, far_count = jnp.transpose(expander_blocks, (1, 2, 0)), jnp.transpose(expander_count)
    tables = (local_blocks, local_count, far_blocks, far_count)
    inputs = (features, w_query, w_key, w_value, w_out, *tables)
    state = (array(rows, width, dtype=jnp.float32),) * 3
    x, w_key, w_value, w_out, queries, bias, times, *states = pl.pallas_call(
        own_kernel,
        out_shape=(
            array(rows, width), *[array(width, width)] * 3, array(rows, width),
            array(match_total + 2, groups, rows, dtype=jnp.float32), array(groups, rows, dtype=jnp.float32),
            *state,
        ),
        in_specs=[ANY] * len(inputs),
        out_specs=(VMEM,) * 10,
        scratch_shapes=[
            pltpu.VMEM((width, width), jnp.bfloat16),
            *pairs_of(rows),
            *(pltpu.SMEM(t.shape, jnp.int32) for t in tables),
            pltpu.SemaphoreType.DMA((len(inputs),)),
        ],
        compiler_params=params,
        name="own",
    )(*(pltpu.with_memory_space_constraint(a, pltpu.HBM) for a in inputs))
    arrived = []
    for one in (before, by_1, by_2, by_3, after):
        one, queries = lax.optimization_barrier((one, queries))
        arrived.append(one)
    before, by_1, by_2, by_3, after = arrived
    return pl.pallas_call(
        rest_kernel,
        out_shape=array(rows, width, dtype=features.dtype),
        in_specs=[VMEM] * 15,
        out_specs=VMEM,
        scratch_shapes=pairs_of(4 * rows + block_rows),
        compiler_params=params,
        name="rest",
    )(x, before, by_1, by_2, by_3, after, w_key, w_value, w_out, queries, bias, times, *states)


def solution(mesh):
    in_specs = (
        P("dom", None),
        P(),
        P(),
        P(),
        P(),
        P("dom", None),
        P("dom"),
        P(None, "dom", None),
        P(None, "dom"),
    )
    out_specs = P("dom", None)
    return jax.shard_map(shards, mesh=mesh, in_specs=in_specs, out_specs=out_specs, check_vma=False)
```

```python
import jax
import jax.numpy as jnp
from jax import lax
from jax.experimental import pallas as pl
from jax.experimental.pallas import tpu as pltpu
from jax.sharding import PartitionSpec as P

HEADS = 8
EPSILON = 1e-06
LOW = -1e30

FIRST = ('own', 'core', 'x')
MIDDLE = ('ring',)
LAST = ('z', 'y')
BIAS_ROW = {"own": 0, "core": 1, "x": 2, "y": 3, "z": 4, "ring": 5}

VMEM = pl.BlockSpec(memory_space=pltpu.VMEM)
ANY = pl.BlockSpec(memory_space=pl.ANY)

def matmul(a, b):
    return jnp.dot(a, b, preferred_element_type=jnp.float32)


def matmul_nt(a, b):
    return lax.dot_general(a, b, (((1,), (1,)), ((), ())), preferred_element_type=jnp.float32)


def used(blocks, count, position, most):
    total = jnp.int32(0)
    for j in range(most):
        total = total + ((blocks(j) == position) & (j < count)).astype(jnp.int32)
    return total


def along_keys(values, block_rows):
    return jnp.concatenate([jnp.full((1, block_rows), v, jnp.float32) for v in values], axis=1)


def attend(queries, parts, groups):
    rows, width = queries.shape
    lanes = width // 2
    count = HEADS // 2
    heads = lax.broadcasted_iota(jnp.int32, (1, lanes), 1) // (lanes // count)
    zero = jnp.zeros((), queries.dtype)

    def by_group(array):
        return array.reshape(count, groups, rows // groups, array.shape[-1])

    cuts = [slice(0, lanes), slice(lanes, width)]
    masked = [
        jnp.concatenate([jnp.where(heads == h, queries[:, cut], zero) for h in range(count)], axis=0) for cut in cuts
    ]
    scores, tops, sums = [[], []], [None, None], [None, None]
    for keys, _, bias, _ in parts:
        for f, cut in enumerate(cuts):
            part = by_group(matmul_nt(masked[f], keys()[:, cut])) + bias()[None, :, None, :]
            part = part.reshape(count * rows, part.shape[-1])
            scores[f].append(part)
            top = jnp.max(part, axis=1, keepdims=True)
            tops[f] = top if tops[f] is None else jnp.maximum(tops[f], top)
    for i, (_, values, _, times) in enumerate(parts):
        for f, cut in enumerate(cuts):
            weights = jnp.exp(scores[f][i] - tops[f])
            if times is not None:
                weights = (by_group(weights) * times()[None, :, None, :]).reshape(weights.shape)
            weights = weights.astype(jnp.bfloat16)
            right = values()[:, cut]
            right = jnp.concatenate([right, jnp.ones_like(right)], axis=1)
            sums[f] = matmul(weights, right) if sums[f] is None else sums[f] + matmul(weights, right)
    state = [[], [], []]
    for f in range(2):
        top = out = total = None
        for h in range(count):
            block = sums[f][h * rows : (h + 1) * rows]
            one = jnp.broadcast_to(tops[f][h * rows : (h + 1) * rows], (rows, lanes)), block[:, :lanes], block[:, lanes:]
            if h == 0:
                top, out, total = one
            else:
                top, out, total = (jnp.where(heads == h, new, old) for new, old in zip(one, (top, out, total)))
        for array, half in zip(state, (top, out, total)):
            array.append(half)
    return tuple(jnp.concatenate(halves, axis=1) for halves in state)


def merge(one, other):
    top = jnp.maximum(one[0], other[0])
    left, right = jnp.exp(one[0] - top), jnp.exp(other[0] - top)
    return top, left * one[1] + right * other[1], left * one[2] + right * other[2]


def project(features, w_key, w_value, keys, values, start):
    rows = pl.ds(start, features.shape[0])
    keys[rows, :] = matmul(features, w_key[...]).astype(keys.dtype)
    values[rows, :] = matmul(features, w_value[...]).astype(values.dtype)


def parts_of(kinds, refs, w_key, w_value, bias, times, keys, values):
    rows = refs[0].shape[0]
    groups = times.shape[0]
    block_rows = rows // groups
    parts = []
    start = 0
    for kind, ref in zip(kinds, refs):
        count = block_rows if kind == "ring" else rows
        if kind == "ring":
            is_odd = lax.rem(lax.axis_index("dom"), 2) == 1
            first = pl.multiple_of(jnp.where(is_odd, 0, rows - block_rows), block_rows)
            arrival = ref[pl.ds(first, block_rows), :]
        else:
            arrival = ref[...]
        project(arrival, w_key, w_value, keys, values, start)
        where = pl.ds(start, count)
        row = BIAS_ROW[kind]
        parts.append((
            lambda where=where: keys[where, :],
            lambda where=where: values[where, :],
            lambda row=row, count=count: bias[row, :, :count],
            (lambda: times[...]) if kind == "core" else None,
        ))
        start += count
    return parts


def first_kernel(
    features, w_query, w_key, w_value, w_out, local_blocks, local_count, expander_blocks, expander_count, *refs
):
    arrivals, refs = refs[: len(FIRST) - 1], refs[len(FIRST) - 1 :]
    (
        x, key_copy, value_copy, out_copy, queries, bias, times, tops, outs, sums,
        query_copy, keys, values, blocks, count, far_blocks, far_count, sems,
    ) = refs
    pairs = (
        (features, x), (w_query, query_copy), (w_key, key_copy), (w_value, value_copy), (local_blocks, blocks),
        (local_count, count), (expander_blocks, far_blocks), (expander_count, far_count), (w_out, out_copy),
    )
    copies = [pltpu.make_async_copy(a, b, sems.at[i]) for i, (a, b) in enumerate(pairs)]
    for copy in copies:
        copy.start()
    groups, most = blocks.shape
    most_far, matchings = far_blocks.shape[1:]
    rows, width = x.shape
    block_rows = rows // groups
    size = width // HEADS
    is_odd = lax.rem(lax.axis_index("dom"), 2) == 1
    for copy in copies[4:8]:
        copy.wait()
    for g in range(groups):
        near = [used(lambda j: blocks[g, j], count[g], position, most) for position in range(groups + 2)]
        takes = [near[1:-1]]
        for m in range(matchings):
            takes.append(
                [used(lambda j: far_blocks[g, j, m], far_count[g, m], b, most_far) for b in range(groups)]
            )
        takes[1][0] = takes[1][0] + jnp.where(is_odd, 0, near[-1])
        takes[1][-1] = takes[1][-1] + jnp.where(is_odd, near[0], 0)
        takes.append([jnp.where(is_odd, near[-1], near[0])] * groups)
        for p, take in enumerate(takes):
            bias[p, g : g + 1, :] = along_keys([jnp.where(t > 0, 0.0, LOW) for t in take], block_rows)
        times[g : g + 1, :] = along_keys([t.astype(jnp.float32) for t in takes[1]], block_rows)
    for copy in copies[:4]:
        copy.wait()
    q = (matmul(x[...], query_copy[...]) * (float(size) ** -0.5)).astype(jnp.bfloat16)
    queries[...] = q
    parts = parts_of(FIRST, (x, *arrivals), key_copy, value_copy, bias, times, keys, values)
    tops[...], outs[...], sums[...] = attend(q, parts, groups)
    copies[8].wait()


def middle_kernel(*refs):
    arrivals, refs = refs[: len(MIDDLE)], refs[len(MIDDLE) :]
    w_key, w_value, queries, bias, times, tops, outs, sums, new_tops, new_outs, new_sums, keys, values = refs
    parts = parts_of(MIDDLE, arrivals, w_key, w_value, bias, times, keys, values)
    state = attend(queries[...], parts, times.shape[0])
    new_tops[...], new_outs[...], new_sums[...] = merge((tops[...], outs[...], sums[...]), state)


def last_kernel(*refs):
    arrivals, refs = refs[: len(LAST)], refs[len(LAST) :]
    w_key, w_value, queries, bias, times, tops, outs, sums, features, w_out, result, keys, values = refs
    parts = parts_of(LAST, arrivals, w_key, w_value, bias, times, keys, values)
    state = attend(queries[...], parts, times.shape[0])
    _, out, total = merge((tops[...], outs[...], sums[...]), state)
    context = (out / total).astype(jnp.bfloat16)
    mixed = matmul(context, w_out[...])
    normed = mixed * lax.rsqrt(jnp.mean(mixed * mixed, axis=1, keepdims=True) + EPSILON)
    result[...] = (features[...].astype(jnp.float32) + normed).astype(result.dtype)


def shards(
    features,
    w_query,
    w_key,
    w_value,
    w_out,
    local_blocks,
    local_count,
    expander_blocks,
    expander_count,
):
    rows, width = features.shape
    groups = local_blocks.shape[0]
    block_rows = rows // groups
    peers = lax.axis_size("dom")
    levels = peers.bit_length() - 1
    match_total = expander_blocks.shape[0]
    params = pltpu.CompilerParams(vmem_limit_bytes=48 * 2**20)

    def array(*shape, dtype=jnp.bfloat16):
        return jax.ShapeDtypeStruct(shape, dtype)

    def pairs_of(total):
        return [pltpu.VMEM((total, width), jnp.bfloat16)] * 2

    def exchange(matching):
        apart = 1 << (matching * levels // match_total)
        return lax.ppermute(features, "dom", [(i, i ^ apart) for i in range(peers)])

    arrived = {
        "core": exchange(0),
        "x": exchange(1),
        "y": exchange(2),
        "z": exchange(3),
        "ring": lax.ppermute(
            features, "dom", [(i, (i + 1) % peers if i % 2 else (i - 1) % peers) for i in range(peers)]
        ),
    }

    def in_order(kinds, after):
        gathered = []
        for kind in kinds:
            one, after = lax.optimization_barrier((arrived[kind], after))
            gathered.append(one)
        return gathered, after

    far_blocks, far_count = jnp.transpose(expander_blocks, (1, 2, 0)), jnp.transpose(expander_count)
    state = (array(rows, width, dtype=jnp.float32),) * 3
    tables = (local_blocks, local_count, far_blocks, far_count)
    inputs = (features, w_query, w_key, w_value, w_out, *tables)
    near, _ = in_order(FIRST[1:], features)
    x, w_key, w_value, w_out, queries, bias, times, *states = pl.pallas_call(
        first_kernel,
        out_shape=(
            array(rows, width), *[array(width, width)] * 3, array(rows, width),
            array(match_total + 2, groups, rows, dtype=jnp.float32), array(groups, rows, dtype=jnp.float32),
            *state,
        ),
        in_specs=[ANY] * len(inputs) + [VMEM] * len(near),
        out_specs=(VMEM,) * 10,
        scratch_shapes=[
            pltpu.VMEM((width, width), jnp.bfloat16),
            *pairs_of(len(FIRST) * rows),
            *(pltpu.SMEM(t.shape, jnp.int32) for t in tables),
            pltpu.SemaphoreType.DMA((len(inputs),)),
        ],
        compiler_params=params,
        name="first",
    )(*(pltpu.with_memory_space_constraint(a, pltpu.HBM) for a in inputs), *near)
    near, queries = in_order(MIDDLE, queries)
    states = pl.pallas_call(
        middle_kernel,
        out_shape=state,
        in_specs=[VMEM] * (len(near) + 8),
        out_specs=(VMEM,) * 3,
        scratch_shapes=pairs_of(len(MIDDLE) * rows),
        compiler_params=params,
        name="middle",
    )(*near, w_key, w_value, queries, bias, times, *states)
    near, states = in_order(LAST, states)
    return pl.pallas_call(
        last_kernel,
        out_shape=array(rows, width, dtype=features.dtype),
        in_specs=[VMEM] * (len(near) + 10),
        out_specs=VMEM,
        scratch_shapes=pairs_of(len(LAST) * rows),
        compiler_params=params,
        name="last",
    )(*near, w_key, w_value, queries, bias, times, *states, x, w_out)


def solution(mesh):
    in_specs = (
        P("dom", None),
        P(),
        P(),
        P(),
        P(),
        P("dom", None),
        P("dom"),
        P(None, "dom", None),
        P(None, "dom"),
    )
    out_specs = P("dom", None)
    return jax.shard_map(shards, mesh=mesh, in_specs=in_specs, out_specs=out_specs, check_vma=False)
```

```python
import functools

import jax
import jax.numpy as jnp
from jax import lax
from jax.experimental import pallas as pl
from jax.experimental.pallas import tpu as pltpu
from jax.sharding import PartitionSpec as P

HEADS = 8
EPSILON = 1e-06
LOW = -1e30

FIRST = ('own',)
MIDDLE = (('core', 'y'), ('ring',))
LAST = ('x', 'z')
BIAS_ROW = {"own": 0, "core": 1, "x": 2, "y": 3, "z": 4, "ring": 5}

VMEM = pl.BlockSpec(memory_space=pltpu.VMEM)
ANY = pl.BlockSpec(memory_space=pl.ANY)

def matmul(a, b):
    return jnp.dot(a, b, preferred_element_type=jnp.float32)


def matmul_nt(a, b):
    return lax.dot_general(a, b, (((1,), (1,)), ((), ())), preferred_element_type=jnp.float32)


def used(blocks, count, position, most):
    total = jnp.int32(0)
    for j in range(most):
        total = total + ((blocks(j) == position) & (j < count)).astype(jnp.int32)
    return total


def along_keys(values, block_rows):
    return jnp.concatenate([jnp.full((1, block_rows), v, jnp.float32) for v in values], axis=1)


def attend(queries, parts, groups):
    rows, width = queries.shape
    lanes = width // 2
    count = HEADS // 2
    heads = lax.broadcasted_iota(jnp.int32, (1, lanes), 1) // (lanes // count)
    zero = jnp.zeros((), queries.dtype)

    def by_group(array):
        return array.reshape(count, groups, rows // groups, array.shape[-1])

    cuts = [slice(0, lanes), slice(lanes, width)]
    masked = [
        jnp.concatenate([jnp.where(heads == h, queries[:, cut], zero) for h in range(count)], axis=0) for cut in cuts
    ]
    scores, tops, sums = [[], []], [None, None], [None, None]
    for f, cut in enumerate(cuts):
        for keys, _, bias, _ in parts:
            part = by_group(matmul_nt(masked[f], keys()[:, cut])) + bias()[None, :, None, :]
            part = part.reshape(count * rows, part.shape[-1])
            scores[f].append(part)
            top = jnp.max(part, axis=1, keepdims=True)
            tops[f] = top if tops[f] is None else jnp.maximum(tops[f], top)
    for f, cut in enumerate(cuts):
        for i, (_, values, _, times) in enumerate(parts):
            weights = jnp.exp(scores[f][i] - tops[f])
            if times is not None:
                weights = (by_group(weights) * times()[None, :, None, :]).reshape(weights.shape)
            weights = weights.astype(jnp.bfloat16)
            right = values()[:, cut]
            right = jnp.concatenate([right, jnp.ones_like(right)], axis=1)
            sums[f] = matmul(weights, right) if sums[f] is None else sums[f] + matmul(weights, right)
    state = [[], [], []]
    for f in range(2):
        top = out = total = None
        for h in range(count):
            block = sums[f][h * rows : (h + 1) * rows]
            one = jnp.broadcast_to(tops[f][h * rows : (h + 1) * rows], (rows, lanes)), block[:, :lanes], block[:, lanes:]
            if h == 0:
                top, out, total = one
            else:
                top, out, total = (jnp.where(heads == h, new, old) for new, old in zip(one, (top, out, total)))
        for array, half in zip(state, (top, out, total)):
            array.append(half)
    return tuple(jnp.concatenate(halves, axis=1) for halves in state)


def merge(one, other):
    top = jnp.maximum(one[0], other[0])
    left, right = jnp.exp(one[0] - top), jnp.exp(other[0] - top)
    return top, left * one[1] + right * other[1], left * one[2] + right * other[2]


def project(features, w_key, w_value, keys, values, start):
    rows = pl.ds(start, features.shape[0])
    keys[rows, :] = matmul(features, w_key[...]).astype(keys.dtype)
    values[rows, :] = matmul(features, w_value[...]).astype(values.dtype)


def parts_of(kinds, refs, w_key, w_value, bias, times, keys, values):
    rows = refs[0].shape[0]
    groups = times.shape[0]
    block_rows = rows // groups
    parts = []
    start = 0
    for kind, ref in zip(kinds, refs):
        count = block_rows if kind == "ring" else rows
        if kind == "ring":
            is_odd = lax.rem(lax.axis_index("dom"), 2) == 1
            first = pl.multiple_of(jnp.where(is_odd, 0, rows - block_rows), block_rows)
            arrival = ref[pl.ds(first, block_rows), :]
        else:
            arrival = ref[...]
        project(arrival, w_key, w_value, keys, values, start)
        where = pl.ds(start, count)
        row = BIAS_ROW[kind]
        parts.append((
            lambda where=where: keys[where, :],
            lambda where=where: values[where, :],
            lambda row=row, count=count: bias[row, :, :count],
            (lambda: times[...]) if kind == "core" else None,
        ))
        start += count
    return parts


def first_kernel(
    features, w_query, w_key, w_value, w_out, local_blocks, local_count, expander_blocks, expander_count, *refs
):
    arrivals, refs = refs[: len(FIRST) - 1], refs[len(FIRST) - 1 :]
    (
        x, key_copy, value_copy, out_copy, queries, bias, times, tops, outs, sums,
        query_copy, keys, values, blocks, count, far_blocks, far_count, sems,
    ) = refs
    pairs = (
        (features, x), (w_query, query_copy), (w_key, key_copy), (w_value, value_copy), (local_blocks, blocks),
        (local_count, count), (expander_blocks, far_blocks), (expander_count, far_count), (w_out, out_copy),
    )
    copies = [pltpu.make_async_copy(a, b, sems.at[i]) for i, (a, b) in enumerate(pairs)]
    for copy in copies:
        copy.start()
    groups, most = blocks.shape
    most_far, matchings = far_blocks.shape[1:]
    rows, width = x.shape
    block_rows = rows // groups
    size = width // HEADS
    is_odd = lax.rem(lax.axis_index("dom"), 2) == 1
    for copy in copies[4:8]:
        copy.wait()
    for g in range(groups):
        near = [used(lambda j: blocks[g, j], count[g], position, most) for position in range(groups + 2)]
        takes = [near[1:-1]]
        for m in range(matchings):
            takes.append(
                [used(lambda j: far_blocks[g, j, m], far_count[g, m], b, most_far) for b in range(groups)]
            )
        takes[1][0] = takes[1][0] + jnp.where(is_odd, 0, near[-1])
        takes[1][-1] = takes[1][-1] + jnp.where(is_odd, near[0], 0)
        takes.append([jnp.where(is_odd, near[-1], near[0])] * groups)
        for p, take in enumerate(takes):
            bias[p, g : g + 1, :] = along_keys([jnp.where(t > 0, 0.0, LOW) for t in take], block_rows)
        times[g : g + 1, :] = along_keys([t.astype(jnp.float32) for t in takes[1]], block_rows)
    for copy in copies[:4]:
        copy.wait()
    q = (matmul(x[...], query_copy[...]) * (float(size) ** -0.5)).astype(jnp.bfloat16)
    queries[...] = q
    parts = parts_of(FIRST, (x, *arrivals), key_copy, value_copy, bias, times, keys, values)
    tops[...], outs[...], sums[...] = attend(q, parts, groups)
    copies[8].wait()


def middle_kernel(kinds, *refs):
    arrivals, refs = refs[: len(kinds)], refs[len(kinds) :]
    w_key, w_value, queries, bias, times, tops, outs, sums, new_tops, new_outs, new_sums, keys, values = refs
    parts = parts_of(kinds, arrivals, w_key, w_value, bias, times, keys, values)
    state = attend(queries[...], parts, times.shape[0])
    new_tops[...], new_outs[...], new_sums[...] = merge((tops[...], outs[...], sums[...]), state)


def last_kernel(*refs):
    arrivals, refs = refs[: len(LAST)], refs[len(LAST) :]
    w_key, w_value, queries, bias, times, tops, outs, sums, features, w_out, result, keys, values = refs
    parts = parts_of(LAST, arrivals, w_key, w_value, bias, times, keys, values)
    state = attend(queries[...], parts, times.shape[0])
    _, out, total = merge((tops[...], outs[...], sums[...]), state)
    context = (out / total).astype(jnp.bfloat16)
    mixed = matmul(context, w_out[...])
    normed = mixed * lax.rsqrt(jnp.mean(mixed * mixed, axis=1, keepdims=True) + EPSILON)
    result[...] = (features[...].astype(jnp.float32) + normed).astype(result.dtype)


def shards(
    features,
    w_query,
    w_key,
    w_value,
    w_out,
    local_blocks,
    local_count,
    expander_blocks,
    expander_count,
):
    rows, width = features.shape
    groups = local_blocks.shape[0]
    block_rows = rows // groups
    peers = lax.axis_size("dom")
    levels = peers.bit_length() - 1
    match_total = expander_blocks.shape[0]
    params = pltpu.CompilerParams(vmem_limit_bytes=48 * 2**20)

    def array(*shape, dtype=jnp.bfloat16):
        return jax.ShapeDtypeStruct(shape, dtype)

    def pairs_of(total):
        return [pltpu.VMEM((total, width), jnp.bfloat16)] * 2

    def exchange(matching):
        apart = 1 << (matching * levels // match_total)
        return lax.ppermute(features, "dom", [(i, i ^ apart) for i in range(peers)])

    arrived = {
        "core": exchange(0),
        "x": exchange(1),
        "y": exchange(2),
        "z": exchange(3),
        "ring": lax.ppermute(
            features, "dom", [(i, (i + 1) % peers if i % 2 else (i - 1) % peers) for i in range(peers)]
        ),
    }

    def in_order(kinds, after):
        gathered = []
        for kind in kinds:
            one, after = lax.optimization_barrier((arrived[kind], after))
            gathered.append(one)
        return gathered, after

    far_blocks, far_count = jnp.transpose(expander_blocks, (1, 2, 0)), jnp.transpose(expander_count)
    state = (array(rows, width, dtype=jnp.float32),) * 3
    tables = (local_blocks, local_count, far_blocks, far_count)
    inputs = (features, w_query, w_key, w_value, w_out, *tables)
    near, _ = in_order(FIRST[1:], features)
    x, w_key, w_value, w_out, queries, bias, times, *states = pl.pallas_call(
        first_kernel,
        out_shape=(
            array(rows, width), *[array(width, width)] * 3, array(rows, width),
            array(match_total + 2, groups, rows, dtype=jnp.float32), array(groups, rows, dtype=jnp.float32),
            *state,
        ),
        in_specs=[ANY] * len(inputs) + [VMEM] * len(near),
        out_specs=(VMEM,) * 10,
        scratch_shapes=[
            pltpu.VMEM((width, width), jnp.bfloat16),
            *pairs_of(len(FIRST) * rows),
            *(pltpu.SMEM(t.shape, jnp.int32) for t in tables),
            pltpu.SemaphoreType.DMA((len(inputs),)),
        ],
        compiler_params=params,
        name="first",
    )(*(pltpu.with_memory_space_constraint(a, pltpu.HBM) for a in inputs), *near)
    for kinds in MIDDLE:
        near, states = in_order(kinds, states)
        states = pl.pallas_call(
            functools.partial(middle_kernel, kinds),
            out_shape=state,
            in_specs=[VMEM] * (len(near) + 8),
            out_specs=(VMEM,) * 3,
            scratch_shapes=pairs_of(len(kinds) * rows),
            compiler_params=params,
            name="_".join(kinds),
        )(*near, w_key, w_value, queries, bias, times, *states)
    near, states = in_order(LAST, states)
    return pl.pallas_call(
        last_kernel,
        out_shape=array(rows, width, dtype=features.dtype),
        in_specs=[VMEM] * (len(near) + 10),
        out_specs=VMEM,
        scratch_shapes=pairs_of(len(LAST) * rows),
        compiler_params=params,
        name="last",
    )(*near, w_key, w_value, queries, bias, times, *states, x, w_out)


def solution(mesh):
    in_specs = (
        P("dom", None),
        P(),
        P(),
        P(),
        P(),
        P("dom", None),
        P("dom"),
        P(None, "dom", None),
        P(None, "dom"),
    )
    out_specs = P("dom", None)
    return jax.shard_map(shards, mesh=mesh, in_specs=in_specs, out_specs=out_specs, check_vma=False)
```

```python
import functools

import jax
import jax.numpy as jnp
from jax import lax
from jax.experimental import pallas as pl
from jax.experimental.pallas import tpu as pltpu
from jax.sharding import PartitionSpec as P

HEADS = 8
EPSILON = 1e-06
LOW = -1e30

FIRST = ("own", "core")
MIDDLE = (("ring", "y"),)
LAST = ("z", "x")
BIAS_ROW = {"own": 0, "core": 1, "x": 2, "y": 3, "z": 4, "ring": 5}

VMEM = pl.BlockSpec(memory_space=pltpu.VMEM)
ANY = pl.BlockSpec(memory_space=pl.ANY)

def matmul(a, b):
    return jnp.dot(a, b, preferred_element_type=jnp.float32)


def matmul_nt(a, b):
    return lax.dot_general(a, b, (((1,), (1,)), ((), ())), preferred_element_type=jnp.float32)


def used(blocks, count, position, most):
    total = jnp.int32(0)
    for j in range(most):
        total = total + ((blocks(j) == position) & (j < count)).astype(jnp.int32)
    return total


def along_keys(values, block_rows):
    return jnp.concatenate([jnp.full((1, block_rows), v, jnp.float32) for v in values], axis=1)


def attend(queries, parts, groups):
    rows, width = queries.shape
    lanes = width // 2
    count = HEADS // 2
    heads = lax.broadcasted_iota(jnp.int32, (1, lanes), 1) // (lanes // count)
    zero = jnp.zeros((), queries.dtype)

    def by_group(array):
        return array.reshape(count, groups, rows // groups, array.shape[-1])

    cuts = [slice(0, lanes), slice(lanes, width)]
    masked = [
        jnp.concatenate([jnp.where(heads == h, queries[:, cut], zero) for h in range(count)], axis=0) for cut in cuts
    ]
    scores, tops, sums = [[], []], [None, None], [None, None]
    for f, cut in enumerate(cuts):
        for keys, _, bias, _ in parts:
            part = by_group(matmul_nt(masked[f], keys()[:, cut])) + bias()[None, :, None, :]
            part = part.reshape(count * rows, part.shape[-1])
            scores[f].append(part)
            top = jnp.max(part, axis=1, keepdims=True)
            tops[f] = top if tops[f] is None else jnp.maximum(tops[f], top)
    for f, cut in enumerate(cuts):
        for i, (_, values, _, times) in enumerate(parts):
            weights = jnp.exp(scores[f][i] - tops[f])
            if times is not None:
                weights = (by_group(weights) * times()[None, :, None, :]).reshape(weights.shape)
            weights = weights.astype(jnp.bfloat16)
            right = values()[:, cut]
            right = jnp.concatenate([right, jnp.ones_like(right)], axis=1)
            sums[f] = matmul(weights, right) if sums[f] is None else sums[f] + matmul(weights, right)
    state = [[], [], []]
    for f in range(2):
        top = out = total = None
        for h in range(count):
            block = sums[f][h * rows : (h + 1) * rows]
            one = jnp.broadcast_to(tops[f][h * rows : (h + 1) * rows], (rows, lanes)), block[:, :lanes], block[:, lanes:]
            if h == 0:
                top, out, total = one
            else:
                top, out, total = (jnp.where(heads == h, new, old) for new, old in zip(one, (top, out, total)))
        for array, half in zip(state, (top, out, total)):
            array.append(half)
    return tuple(jnp.concatenate(halves, axis=1) for halves in state)


def merge(one, other):
    top = jnp.maximum(one[0], other[0])
    left, right = jnp.exp(one[0] - top), jnp.exp(other[0] - top)
    return top, left * one[1] + right * other[1], left * one[2] + right * other[2]


def project(features, w_key, w_value, keys, values, start):
    rows = pl.ds(start, features.shape[0])
    keys[rows, :] = matmul(features, w_key[...]).astype(keys.dtype)
    values[rows, :] = matmul(features, w_value[...]).astype(values.dtype)


def parts_of(kinds, refs, w_key, w_value, bias, times, keys, values, swapped=()):
    rows = refs[0].shape[0]
    groups = times.shape[0]
    block_rows = rows // groups
    parts = []
    start = 0
    me = lax.axis_index("dom")
    is_swapped = functools.reduce(lambda one, device: one | (me == device), swapped, me < 0)
    named = dict(zip(kinds, refs))
    for kind, ref in zip(kinds, refs):
        count = block_rows if kind == "ring" else rows
        if kind == "ring":
            is_odd = lax.rem(me, 2) == 1
            first = pl.multiple_of(jnp.where(is_odd, 0, rows - block_rows), block_rows)
            where = pl.ds(first, block_rows)
            arrival = jnp.where(is_swapped, named["y"][where, :], ref[where, :])
        elif kind == "y":
            arrival = jnp.where(is_swapped, named["ring"][...], ref[...])
        else:
            arrival = ref[...]
        project(arrival, w_key, w_value, keys, values, start)
        where = pl.ds(start, count)
        row = BIAS_ROW[kind]
        parts.append((
            lambda where=where: keys[where, :],
            lambda where=where: values[where, :],
            lambda row=row, count=count: bias[row, :, :count],
            (lambda: times[...]) if kind == "core" else None,
        ))
        start += count
    return parts


def first_kernel(
    features, w_query, w_key, w_value, w_out, local_blocks, local_count, expander_blocks, expander_count, *refs
):
    arrivals, refs = refs[: len(FIRST) - 1], refs[len(FIRST) - 1 :]
    (
        x, key_copy, value_copy, out_copy, queries, bias, times, tops, outs, sums,
        query_copy, keys, values, blocks, count, far_blocks, far_count, sems,
    ) = refs
    pairs = (
        (features, x), (w_query, query_copy), (w_key, key_copy), (w_value, value_copy), (local_blocks, blocks),
        (local_count, count), (expander_blocks, far_blocks), (expander_count, far_count), (w_out, out_copy),
    )
    copies = [pltpu.make_async_copy(a, b, sems.at[i]) for i, (a, b) in enumerate(pairs)]
    for copy in copies:
        copy.start()
    groups, most = blocks.shape
    most_far, matchings = far_blocks.shape[1:]
    rows, width = x.shape
    block_rows = rows // groups
    size = width // HEADS
    is_odd = lax.rem(lax.axis_index("dom"), 2) == 1
    for copy in copies[4:8]:
        copy.wait()
    for g in range(groups):
        near = [used(lambda j: blocks[g, j], count[g], position, most) for position in range(groups + 2)]
        takes = [near[1:-1]]
        for m in range(matchings):
            takes.append(
                [used(lambda j: far_blocks[g, j, m], far_count[g, m], b, most_far) for b in range(groups)]
            )
        takes[1][0] = takes[1][0] + jnp.where(is_odd, 0, near[-1])
        takes[1][-1] = takes[1][-1] + jnp.where(is_odd, near[0], 0)
        takes.append([jnp.where(is_odd, near[-1], near[0])] * groups)
        for p, take in enumerate(takes):
            bias[p, g : g + 1, :] = along_keys([jnp.where(t > 0, 0.0, LOW) for t in take], block_rows)
        times[g : g + 1, :] = along_keys([t.astype(jnp.float32) for t in takes[1]], block_rows)
    for copy in copies[:4]:
        copy.wait()
    q = (matmul(x[...], query_copy[...]) * (float(size) ** -0.5)).astype(jnp.bfloat16)
    queries[...] = q
    parts = parts_of(FIRST, (x, *arrivals), key_copy, value_copy, bias, times, keys, values)
    tops[...], outs[...], sums[...] = attend(q, parts, groups)
    copies[8].wait()


def middle_kernel(kinds, swapped, *refs):
    arrivals, refs = refs[: len(kinds)], refs[len(kinds) :]
    w_key, w_value, queries, bias, times, tops, outs, sums, new_tops, new_outs, new_sums, keys, values = refs
    parts = parts_of(kinds, arrivals, w_key, w_value, bias, times, keys, values, swapped)
    state = attend(queries[...], parts, times.shape[0])
    new_tops[...], new_outs[...], new_sums[...] = merge((tops[...], outs[...], sums[...]), state)


def last_kernel(*refs):
    arrivals, refs = refs[: len(LAST)], refs[len(LAST) :]
    w_key, w_value, queries, bias, times, tops, outs, sums, features, w_out, result, keys, values = refs
    parts = parts_of(LAST, arrivals, w_key, w_value, bias, times, keys, values)
    state = attend(queries[...], parts, times.shape[0])
    _, out, total = merge((tops[...], outs[...], sums[...]), state)
    context = (out / total).astype(jnp.bfloat16)
    mixed = matmul(context, w_out[...])
    normed = mixed * lax.rsqrt(jnp.mean(mixed * mixed, axis=1, keepdims=True) + EPSILON)
    result[...] = (features[...].astype(jnp.float32) + normed).astype(result.dtype)


def shards(
    features,
    w_query,
    w_key,
    w_value,
    w_out,
    local_blocks,
    local_count,
    expander_blocks,
    expander_count,
):
    rows, width = features.shape
    groups = local_blocks.shape[0]
    block_rows = rows // groups
    peers = lax.axis_size("dom")
    levels = peers.bit_length() - 1
    match_total = expander_blocks.shape[0]
    params = pltpu.CompilerParams(vmem_limit_bytes=48 * 2**20)

    def array(*shape, dtype=jnp.bfloat16):
        return jax.ShapeDtypeStruct(shape, dtype)

    def pairs_of(total):
        return [pltpu.VMEM((total, width), jnp.bfloat16)] * 2

    def exchange(matching):
        apart = 1 << (matching * levels // match_total)
        return lax.ppermute(features, "dom", [(i, i ^ apart) for i in range(peers)])

    ring_of = [(i + 1) % peers if i % 2 else (i - 1) % peers for i in range(peers)]
    far_of = [i ^ (1 << (2 * levels // match_total)) for i in range(peers)]
    swapped = []
    device, end = 0, ring_of[0]
    while end not in swapped:
        ring_of[device], far_of[device] = far_of[device], ring_of[device]
        target = ring_of[device]
        swapped.append(target)
        device = next((i for i in range(peers) if ring_of[i] == target and i != device), None)
    arrived = {
        "core": exchange(0),
        "x": exchange(1),
        "y": lax.ppermute(features, "dom", list(enumerate(far_of))),
        "z": exchange(3),
        "ring": lax.ppermute(features, "dom", list(enumerate(ring_of))),
    }
    swapped = tuple(swapped)

    def in_order(kinds, after):
        gathered = []
        for kind in kinds:
            one, after = lax.optimization_barrier((arrived[kind], after))
            gathered.append(one)
        return gathered, after

    far_blocks, far_count = jnp.transpose(expander_blocks, (1, 2, 0)), jnp.transpose(expander_count)
    state = (array(rows, width, dtype=jnp.float32),) * 3
    tables = (local_blocks, local_count, far_blocks, far_count)
    inputs = (features, w_query, w_key, w_value, w_out, *tables)
    near, _ = in_order(FIRST[1:], features)
    x, w_key, w_value, w_out, queries, bias, times, *states = pl.pallas_call(
        first_kernel,
        out_shape=(
            array(rows, width), *[array(width, width)] * 3, array(rows, width),
            array(match_total + 2, groups, rows, dtype=jnp.float32), array(groups, rows, dtype=jnp.float32),
            *state,
        ),
        in_specs=[ANY] * len(inputs) + [VMEM] * len(near),
        out_specs=(VMEM,) * 10,
        scratch_shapes=[
            pltpu.VMEM((width, width), jnp.bfloat16),
            *pairs_of(len(FIRST) * rows),
            *(pltpu.SMEM(t.shape, jnp.int32) for t in tables),
            pltpu.SemaphoreType.DMA((len(inputs),)),
        ],
        compiler_params=params,
        name="first",
    )(*(pltpu.with_memory_space_constraint(a, pltpu.HBM) for a in inputs), *near)
    for kinds in MIDDLE:
        near, states = in_order(kinds, states)
        states = pl.pallas_call(
            functools.partial(middle_kernel, kinds, swapped),
            out_shape=state,
            in_specs=[VMEM] * (len(near) + 8),
            out_specs=(VMEM,) * 3,
            scratch_shapes=pairs_of(len(kinds) * rows),
            compiler_params=params,
            name="_".join(kinds),
        )(*near, w_key, w_value, queries, bias, times, *states)
    near, states = in_order(LAST, states)
    return pl.pallas_call(
        last_kernel,
        out_shape=array(rows, width, dtype=features.dtype),
        in_specs=[VMEM] * (len(near) + 10),
        out_specs=VMEM,
        scratch_shapes=pairs_of(len(LAST) * rows),
        compiler_params=params,
        name="last",
    )(*near, w_key, w_value, queries, bias, times, *states, x, w_out)


def solution(mesh):
    in_specs = (
        P("dom", None),
        P(),
        P(),
        P(),
        P(),
        P("dom", None),
        P("dom"),
        P(None, "dom", None),
        P(None, "dom"),
    )
    out_specs = P("dom", None)
    return jax.shard_map(shards, mesh=mesh, in_specs=in_specs, out_specs=out_specs, check_vma=False)
```

```python
import functools

import jax
import jax.numpy as jnp
from jax import lax
from jax.experimental import pallas as pl
from jax.experimental.pallas import tpu as pltpu
from jax.sharding import PartitionSpec as P

HEADS = 8
EPSILON = 1e-06
LOW = -1e30

FIRST = ("own", "core")
MIDDLE = (("ring", "y"),)
LAST = ("z", "x")
BIAS_ROW = {"own": 0, "core": 1, "x": 2, "y": 3, "z": 4, "ring": 5}
TIMES_ROW = {"core": 0, "x": 1}

VMEM = pl.BlockSpec(memory_space=pltpu.VMEM)
ANY = pl.BlockSpec(memory_space=pl.ANY)

def matmul(a, b):
    return jnp.dot(a, b, preferred_element_type=jnp.float32)


def matmul_nt(a, b):
    return lax.dot_general(a, b, (((1,), (1,)), ((), ())), preferred_element_type=jnp.float32)


def used(blocks, count, position, most):
    total = jnp.int32(0)
    for j in range(most):
        total = total + ((blocks(j) == position) & (j < count)).astype(jnp.int32)
    return total


def along_keys(values, block_rows):
    return jnp.concatenate([jnp.full((1, block_rows), v, jnp.float32) for v in values], axis=1)


def attend(queries, parts, groups):
    rows, width = queries.shape
    lanes = width // 2
    count = HEADS // 2
    heads = lax.broadcasted_iota(jnp.int32, (1, lanes), 1) // (lanes // count)
    zero = jnp.zeros((), queries.dtype)

    def by_group(array):
        return array.reshape(count, groups, rows // groups, array.shape[-1])

    cuts = [slice(0, lanes), slice(lanes, width)]
    masked = [
        jnp.concatenate([jnp.where(heads == h, queries[:, cut], zero) for h in range(count)], axis=0) for cut in cuts
    ]
    scores, tops, sums = [[], []], [None, None], [None, None]
    for f, cut in enumerate(cuts):
        for keys, _, bias, _ in parts:
            part = by_group(matmul_nt(masked[f], keys()[:, cut])) + bias()[None, :, None, :]
            part = part.reshape(count * rows, part.shape[-1])
            scores[f].append(part)
            top = jnp.max(part, axis=1, keepdims=True)
            tops[f] = top if tops[f] is None else jnp.maximum(tops[f], top)
    for f, cut in enumerate(cuts):
        for i, (_, values, _, times) in enumerate(parts):
            weights = jnp.exp(scores[f][i] - tops[f])
            if times is not None:
                weights = (by_group(weights) * times()[None, :, None, :]).reshape(weights.shape)
            weights = weights.astype(jnp.bfloat16)
            right = values()[:, cut]
            right = jnp.concatenate([right, jnp.ones_like(right)], axis=1)
            sums[f] = matmul(weights, right) if sums[f] is None else sums[f] + matmul(weights, right)
    state = [[], [], []]
    for f in range(2):
        top = out = total = None
        for h in range(count):
            block = sums[f][h * rows : (h + 1) * rows]
            one = jnp.broadcast_to(tops[f][h * rows : (h + 1) * rows], (rows, lanes)), block[:, :lanes], block[:, lanes:]
            if h == 0:
                top, out, total = one
            else:
                top, out, total = (jnp.where(heads == h, new, old) for new, old in zip(one, (top, out, total)))
        for array, half in zip(state, (top, out, total)):
            array.append(half)
    return tuple(jnp.concatenate(halves, axis=1) for halves in state)


def merge(one, other):
    top = jnp.maximum(one[0], other[0])
    left, right = jnp.exp(one[0] - top), jnp.exp(other[0] - top)
    return top, left * one[1] + right * other[1], left * one[2] + right * other[2]


def project(features, w_key, w_value, keys, values, start):
    rows = pl.ds(start, features.shape[0])
    keys[rows, :] = matmul(features, w_key[...]).astype(keys.dtype)
    values[rows, :] = matmul(features, w_value[...]).astype(values.dtype)


def parts_of(kinds, refs, w_key, w_value, bias, times, keys, values, swapped=()):
    rows = refs[0].shape[0]
    groups = times.shape[1]
    block_rows = rows // groups
    parts = []
    start = 0
    me = lax.axis_index("dom")
    is_swapped = functools.reduce(lambda one, device: one | (me == device), swapped, me < 0)
    named = dict(zip(kinds, refs))
    for kind, ref in zip(kinds, refs):
        count = block_rows if kind == "ring" else rows
        if kind == "ring":
            is_odd = lax.rem(me, 2) == 1
            first = pl.multiple_of(jnp.where(is_odd, 0, rows - block_rows), block_rows)
            where = pl.ds(first, block_rows)
            arrival = jnp.where(is_swapped, named["y"][where, :], ref[where, :])
        elif kind == "y":
            arrival = jnp.where(is_swapped, named["ring"][...], ref[...])
        else:
            arrival = ref[...]
        project(arrival, w_key, w_value, keys, values, start)
        where = pl.ds(start, count)
        row, repeats = BIAS_ROW[kind], TIMES_ROW.get(kind)
        parts.append((
            lambda where=where: keys[where, :],
            lambda where=where: values[where, :],
            lambda row=row, count=count: bias[row, :, :count],
            None if repeats is None else lambda repeats=repeats: times[repeats],
        ))
        start += count
    return parts


def matching_apart(peers, matching, match_total):
    return 1 << (matching * (peers.bit_length() - 1) // match_total)


def moved_targets(peers, match_total):
    return (peers - 2, (peers - 1) ^ matching_apart(peers, 1, match_total))


def first_kernel(
    features, w_query, w_key, w_value, w_out, local_blocks, local_count, expander_blocks, expander_count, *refs
):
    arrivals, refs = refs[: len(FIRST) - 1], refs[len(FIRST) - 1 :]
    (
        x, key_copy, value_copy, out_copy, queries, bias, times, tops, outs, sums,
        query_copy, keys, values, blocks, count, far_blocks, far_count, sems,
    ) = refs
    pairs = (
        (features, x), (w_query, query_copy), (w_key, key_copy), (w_value, value_copy), (local_blocks, blocks),
        (local_count, count), (expander_blocks, far_blocks), (expander_count, far_count), (w_out, out_copy),
    )
    copies = [pltpu.make_async_copy(a, b, sems.at[i]) for i, (a, b) in enumerate(pairs)]
    for copy in copies:
        copy.start()
    groups, most = blocks.shape
    most_far, matchings = far_blocks.shape[1:]
    rows, width = x.shape
    block_rows = rows // groups
    size = width // HEADS
    me, peers = lax.axis_index("dom"), lax.axis_size("dom")
    is_odd = lax.rem(me, 2) == 1
    is_moved = functools.reduce(lambda one, device: one | (me == device), moved_targets(peers, matchings), me < 0)
    for copy in copies[4:8]:
        copy.wait()
    for g in range(groups):
        near = [used(lambda j: blocks[g, j], count[g], position, most) for position in range(groups + 2)]
        takes = [near[1:-1]]
        for m in range(matchings):
            takes.append(
                [used(lambda j: far_blocks[g, j, m], far_count[g, m], b, most_far) for b in range(groups)]
            )
        takes[1][0] = takes[1][0] + jnp.where(is_odd, 0, near[-1])
        takes[1][-1] = takes[1][-1] + jnp.where(is_odd, near[0], 0)
        takes.append([jnp.where(is_odd, near[-1], near[0])] * groups)
        takes[1:3] = (
            [jnp.where(is_moved, other, one) for one, other in zip(*pair)]
            for pair in ((takes[1], takes[2]), (takes[2], takes[1]))
        )
        for p, take in enumerate(takes):
            bias[p, g : g + 1, :] = along_keys([jnp.where(t > 0, 0.0, LOW) for t in take], block_rows)
        for i in range(2):
            times[i, g : g + 1, :] = along_keys([t.astype(jnp.float32) for t in takes[1 + i]], block_rows)
    for copy in copies[:4]:
        copy.wait()
    q = (matmul(x[...], query_copy[...]) * (float(size) ** -0.5)).astype(jnp.bfloat16)
    queries[...] = q
    parts = parts_of(FIRST, (x, *arrivals), key_copy, value_copy, bias, times, keys, values)
    tops[...], outs[...], sums[...] = attend(q, parts, groups)
    copies[8].wait()


def middle_kernel(kinds, swapped, *refs):
    arrivals, refs = refs[: len(kinds)], refs[len(kinds) :]
    w_key, w_value, queries, bias, times, tops, outs, sums, new_tops, new_outs, new_sums, keys, values = refs
    parts = parts_of(kinds, arrivals, w_key, w_value, bias, times, keys, values, swapped)
    state = attend(queries[...], parts, times.shape[1])
    new_tops[...], new_outs[...], new_sums[...] = merge((tops[...], outs[...], sums[...]), state)


def last_kernel(*refs):
    arrivals, refs = refs[: len(LAST)], refs[len(LAST) :]
    w_key, w_value, queries, bias, times, tops, outs, sums, features, w_out, result, keys, values = refs
    parts = parts_of(LAST, arrivals, w_key, w_value, bias, times, keys, values)
    state = attend(queries[...], parts, times.shape[1])
    _, out, total = merge((tops[...], outs[...], sums[...]), state)
    context = (out / total).astype(jnp.bfloat16)
    mixed = matmul(context, w_out[...])
    normed = mixed * lax.rsqrt(jnp.mean(mixed * mixed, axis=1, keepdims=True) + EPSILON)
    result[...] = (features[...].astype(jnp.float32) + normed).astype(result.dtype)


def shards(
    features,
    w_query,
    w_key,
    w_value,
    w_out,
    local_blocks,
    local_count,
    expander_blocks,
    expander_count,
):
    rows, width = features.shape
    groups = local_blocks.shape[0]
    block_rows = rows // groups
    peers = lax.axis_size("dom")
    match_total = expander_blocks.shape[0]
    params = pltpu.CompilerParams(vmem_limit_bytes=48 * 2**20)

    def array(*shape, dtype=jnp.bfloat16):
        return jax.ShapeDtypeStruct(shape, dtype)

    def pairs_of(total):
        return [pltpu.VMEM((total, width), jnp.bfloat16)] * 2

    def exchange(matching):
        apart = matching_apart(peers, matching, match_total)
        return lax.ppermute(features, "dom", [(i, i ^ apart) for i in range(peers)])

    ring_of = [(i + 1) % peers if i % 2 else (i - 1) % peers for i in range(peers)]
    far_of = [i ^ matching_apart(peers, 2, match_total) for i in range(peers)]
    swapped = []
    device, end = 0, ring_of[0]
    while end not in swapped:
        ring_of[device], far_of[device] = far_of[device], ring_of[device]
        target = ring_of[device]
        swapped.append(target)
        device = next((i for i in range(peers) if ring_of[i] == target and i != device), None)
    near = matching_apart(peers, 1, match_total)
    core_of, near_of = [i ^ 1 for i in range(peers)], [i ^ near for i in range(peers)]
    for device in (peers - 1, (peers - 1) ^ near ^ 1):
        core_of[device], near_of[device] = near_of[device], core_of[device]
    arrived = {
        "core": lax.ppermute(features, "dom", list(enumerate(core_of))),
        "x": lax.ppermute(features, "dom", list(enumerate(near_of))),
        "y": lax.ppermute(features, "dom", list(enumerate(far_of))),
        "z": exchange(3),
        "ring": lax.ppermute(features, "dom", list(enumerate(ring_of))),
    }
    swapped = tuple(swapped)

    def in_order(kinds, after):
        gathered = []
        for kind in kinds:
            one, after = lax.optimization_barrier((arrived[kind], after))
            gathered.append(one)
        return gathered, after

    far_blocks, far_count = jnp.transpose(expander_blocks, (1, 2, 0)), jnp.transpose(expander_count)
    state = (array(rows, width, dtype=jnp.float32),) * 3
    tables = (local_blocks, local_count, far_blocks, far_count)
    inputs = (features, w_query, w_key, w_value, w_out, *tables)
    near, _ = in_order(FIRST[1:], features)
    x, w_key, w_value, w_out, queries, bias, times, *states = pl.pallas_call(
        first_kernel,
        out_shape=(
            array(rows, width), *[array(width, width)] * 3, array(rows, width),
            array(match_total + 2, groups, rows, dtype=jnp.float32), array(2, groups, rows, dtype=jnp.float32),
            *state,
        ),
        in_specs=[ANY] * len(inputs) + [VMEM] * len(near),
        out_specs=(VMEM,) * 10,
        scratch_shapes=[
            pltpu.VMEM((width, width), jnp.bfloat16),
            *pairs_of(len(FIRST) * rows),
            *(pltpu.SMEM(t.shape, jnp.int32) for t in tables),
            pltpu.SemaphoreType.DMA((len(inputs),)),
        ],
        compiler_params=params,
        name="first",
    )(*(pltpu.with_memory_space_constraint(a, pltpu.HBM) for a in inputs), *near)
    for kinds in MIDDLE:
        near, states = in_order(kinds, states)
        states = pl.pallas_call(
            functools.partial(middle_kernel, kinds, swapped),
            out_shape=state,
            in_specs=[VMEM] * (len(near) + 8),
            out_specs=(VMEM,) * 3,
            scratch_shapes=pairs_of(len(kinds) * rows),
            compiler_params=params,
            name="_".join(kinds),
        )(*near, w_key, w_value, queries, bias, times, *states)
    near, states = in_order(LAST, states)
    return pl.pallas_call(
        last_kernel,
        out_shape=array(rows, width, dtype=features.dtype),
        in_specs=[VMEM] * (len(near) + 10),
        out_specs=VMEM,
        scratch_shapes=pairs_of(len(LAST) * rows),
        compiler_params=params,
        name="last",
    )(*near, w_key, w_value, queries, bias, times, *states, x, w_out)


def solution(mesh):
    in_specs = (
        P("dom", None),
        P(),
        P(),
        P(),
        P(),
        P("dom", None),
        P("dom"),
        P(None, "dom", None),
        P(None, "dom"),
    )
    out_specs = P("dom", None)
    return jax.shard_map(shards, mesh=mesh, in_specs=in_specs, out_specs=out_specs, check_vma=False)
```

```python
import functools

import jax
import jax.numpy as jnp
from jax import lax
from jax.experimental import pallas as pl
from jax.experimental.pallas import tpu as pltpu
from jax.sharding import PartitionSpec as P

HEADS = 8
EPSILON = 1e-06
LOW = -1e30

FIRST = ("own", "core")
MIDDLE = (("ring", "y"),)
LAST = ("z", "x")
BIAS_ROW = {"own": 0, "core": 1, "x": 2, "y": 3, "z": 4, "ring": 5}
TIMES_ROW = {"core": 0, "x": 1}

VMEM = pl.BlockSpec(memory_space=pltpu.VMEM)
ANY = pl.BlockSpec(memory_space=pl.ANY)

def matmul(a, b):
    return jnp.dot(a, b, preferred_element_type=jnp.float32)


def matmul_nt(a, b):
    return lax.dot_general(a, b, (((1,), (1,)), ((), ())), preferred_element_type=jnp.float32)


def used(blocks, count, position, most):
    total = jnp.int32(0)
    for j in range(most):
        total = total + ((blocks(j) == position) & (j < count)).astype(jnp.int32)
    return total


def along_keys(values, block_rows):
    return jnp.concatenate([jnp.full((1, block_rows), v, jnp.float32) for v in values], axis=1)


def attend(queries, parts, groups):
    rows, width = queries.shape
    lanes = width // 2
    count = HEADS // 2
    heads = lax.broadcasted_iota(jnp.int32, (1, lanes), 1) // (lanes // count)
    zero = jnp.zeros((), queries.dtype)

    def by_group(array):
        return array.reshape(count, groups, rows // groups, array.shape[-1])

    cuts = [slice(0, lanes), slice(lanes, width)]
    row_group = lax.broadcasted_iota(jnp.int32, (rows, lanes), 0) // (rows // groups)
    chooses = (row_group == lax.broadcasted_iota(jnp.int32, (rows, lanes), 1)).astype(queries.dtype)
    masked = [
        jnp.concatenate(
            [jnp.concatenate([jnp.where(heads == h, queries[:, cut], zero), chooses], axis=1) for h in range(count)],
            axis=0,
        )
        for cut in cuts
    ]
    scores, tops, sums = [[], []], [None, None], [None, None]
    for f in range(2):
        for keys, _, _ in parts:
            part = matmul_nt(masked[f], keys(f))
            scores[f].append(part)
            top = jnp.max(part, axis=1, keepdims=True)
            tops[f] = top if tops[f] is None else jnp.maximum(tops[f], top)
    for f, cut in enumerate(cuts):
        for i, (_, values, times) in enumerate(parts):
            weights = jnp.exp(scores[f][i] - tops[f])
            if times is not None:
                weights = (by_group(weights) * times()[None, :, None, :]).reshape(weights.shape)
            weights = weights.astype(jnp.bfloat16)
            right = values()[:, cut]
            right = jnp.concatenate([right, jnp.ones_like(right)], axis=1)
            sums[f] = matmul(weights, right) if sums[f] is None else sums[f] + matmul(weights, right)
    state = [[], [], []]
    for f in range(2):
        top = out = total = None
        for h in range(count):
            block = sums[f][h * rows : (h + 1) * rows]
            one = jnp.broadcast_to(tops[f][h * rows : (h + 1) * rows], (rows, lanes)), block[:, :lanes], block[:, lanes:]
            if h == 0:
                top, out, total = one
            else:
                top, out, total = (jnp.where(heads == h, new, old) for new, old in zip(one, (top, out, total)))
        for array, half in zip(state, (top, out, total)):
            array.append(half)
    return tuple(jnp.concatenate(halves, axis=1) for halves in state)


def merge(one, other):
    top = jnp.maximum(one[0], other[0])
    left, right = jnp.exp(one[0] - top), jnp.exp(other[0] - top)
    return top, left * one[1] + right * other[1], left * one[2] + right * other[2]


def project(features, w_key, w_value, keys, values, start):
    rows = pl.ds(start, features.shape[0])
    lanes = keys.shape[1] // 4
    made = matmul(features, w_key[...]).astype(keys.dtype)
    keys[rows, pl.ds(0, lanes)] = made[:, :lanes]
    keys[rows, pl.ds(2 * lanes, lanes)] = made[:, lanes:]
    values[rows, :] = matmul(features, w_value[...]).astype(values.dtype)


def parts_of(kinds, refs, w_key, w_value, bias, times, keys, values, swapped=()):
    rows = refs[0].shape[0]
    groups = times.shape[1]
    block_rows = rows // groups
    parts = []
    start = 0
    me = lax.axis_index("dom")
    is_swapped = functools.reduce(lambda one, device: one | (me == device), swapped, me < 0)
    named = dict(zip(kinds, refs))
    for kind, ref in zip(kinds, refs):
        count = block_rows if kind == "ring" else rows
        if kind == "ring":
            is_odd = lax.rem(me, 2) == 1
            first = pl.multiple_of(jnp.where(is_odd, 0, rows - block_rows), block_rows)
            where = pl.ds(first, block_rows)
            arrival = jnp.where(is_swapped, named["y"][where, :], ref[where, :])
        elif kind == "y":
            arrival = jnp.where(is_swapped, named["ring"][...], ref[...])
        else:
            arrival = ref[...]
        row, repeats = BIAS_ROW[kind], TIMES_ROW.get(kind)
        project(arrival, w_key, w_value, keys, values, start)
        lanes = keys.shape[1] // 4
        lane = lax.broadcasted_iota(jnp.int32, (1, lanes), 1)
        for b in range(count // block_rows):
            mask = jnp.zeros((1, lanes), jnp.float32)
            for g in range(groups):
                mask = jnp.where(lane == g, bias[row, g : g + 1, b * block_rows : b * block_rows + 1], mask)
            mask = jnp.broadcast_to(mask.astype(keys.dtype), (block_rows, lanes))
            for f in range(2):
                keys[pl.ds(start + b * block_rows, block_rows), pl.ds((2 * f + 1) * lanes, lanes)] = mask
        where = pl.ds(start, count)
        parts.append((
            lambda f, where=where: keys[where, pl.ds(f * keys.shape[1] // 2, keys.shape[1] // 2)],
            lambda where=where: values[where, :],
            None if repeats is None else lambda repeats=repeats: times[repeats],
        ))
        start += count
    return parts


def matching_apart(peers, matching, match_total):
    return 1 << (matching * (peers.bit_length() - 1) // match_total)


def moved_targets(peers, match_total):
    return (peers - 2, (peers - 1) ^ matching_apart(peers, 1, match_total))


def first_kernel(
    features, w_query, w_key, w_value, w_out, local_blocks, local_count, expander_blocks, expander_count, *refs
):
    arrivals, refs = refs[: len(FIRST) - 1], refs[len(FIRST) - 1 :]
    (
        x, key_copy, value_copy, out_copy, queries, bias, times, tops, outs, sums,
        query_copy, keys, values, blocks, count, far_blocks, far_count, sems,
    ) = refs
    pairs = (
        (features, x), (w_query, query_copy), (w_key, key_copy), (w_value, value_copy), (local_blocks, blocks),
        (local_count, count), (expander_blocks, far_blocks), (expander_count, far_count), (w_out, out_copy),
    )
    copies = [pltpu.make_async_copy(a, b, sems.at[i]) for i, (a, b) in enumerate(pairs)]
    for copy in copies:
        copy.start()
    groups, most = blocks.shape
    most_far, matchings = far_blocks.shape[1:]
    rows, width = x.shape
    block_rows = rows // groups
    size = width // HEADS
    me, peers = lax.axis_index("dom"), lax.axis_size("dom")
    is_odd = lax.rem(me, 2) == 1
    is_moved = functools.reduce(lambda one, device: one | (me == device), moved_targets(peers, matchings), me < 0)
    for copy in copies[4:8]:
        copy.wait()
    for g in range(groups):
        near = [used(lambda j: blocks[g, j], count[g], position, most) for position in range(groups + 2)]
        takes = [near[1:-1]]
        for m in range(matchings):
            takes.append(
                [used(lambda j: far_blocks[g, j, m], far_count[g, m], b, most_far) for b in range(groups)]
            )
        takes[1][0] = takes[1][0] + jnp.where(is_odd, 0, near[-1])
        takes[1][-1] = takes[1][-1] + jnp.where(is_odd, near[0], 0)
        takes.append([jnp.where(is_odd, near[-1], near[0])] * groups)
        takes[1:3] = (
            [jnp.where(is_moved, other, one) for one, other in zip(*pair)]
            for pair in ((takes[1], takes[2]), (takes[2], takes[1]))
        )
        for p, take in enumerate(takes):
            bias[p, g : g + 1, :] = along_keys([jnp.where(t > 0, 0.0, LOW) for t in take], block_rows)
        for i in range(2):
            times[i, g : g + 1, :] = along_keys([t.astype(jnp.float32) for t in takes[1 + i]], block_rows)
    for copy in copies[:4]:
        copy.wait()
    q = (matmul(x[...], query_copy[...]) * (float(size) ** -0.5)).astype(jnp.bfloat16)
    queries[...] = q
    parts = parts_of(FIRST, (x, *arrivals), key_copy, value_copy, bias, times, keys, values)
    tops[...], outs[...], sums[...] = attend(q, parts, groups)
    copies[8].wait()


def middle_kernel(kinds, swapped, *refs):
    arrivals, refs = refs[: len(kinds)], refs[len(kinds) :]
    w_key, w_value, queries, bias, times, tops, outs, sums, new_tops, new_outs, new_sums, keys, values = refs
    parts = parts_of(kinds, arrivals, w_key, w_value, bias, times, keys, values, swapped)
    state = attend(queries[...], parts, times.shape[1])
    new_tops[...], new_outs[...], new_sums[...] = merge((tops[...], outs[...], sums[...]), state)


def last_kernel(*refs):
    arrivals, refs = refs[: len(LAST)], refs[len(LAST) :]
    w_key, w_value, queries, bias, times, tops, outs, sums, features, w_out, result, keys, values = refs
    parts = parts_of(LAST, arrivals, w_key, w_value, bias, times, keys, values)
    state = attend(queries[...], parts, times.shape[1])
    _, out, total = merge((tops[...], outs[...], sums[...]), state)
    context = (out / total).astype(jnp.bfloat16)
    mixed = matmul(context, w_out[...])
    normed = mixed * lax.rsqrt(jnp.mean(mixed * mixed, axis=1, keepdims=True) + EPSILON)
    result[...] = (features[...].astype(jnp.float32) + normed).astype(result.dtype)


def shards(
    features,
    w_query,
    w_key,
    w_value,
    w_out,
    local_blocks,
    local_count,
    expander_blocks,
    expander_count,
):
    rows, width = features.shape
    groups = local_blocks.shape[0]
    block_rows = rows // groups
    peers = lax.axis_size("dom")
    match_total = expander_blocks.shape[0]
    params = pltpu.CompilerParams(vmem_limit_bytes=48 * 2**20)

    def array(*shape, dtype=jnp.bfloat16):
        return jax.ShapeDtypeStruct(shape, dtype)

    def pairs_of(total):
        return [pltpu.VMEM((total, 2 * width), jnp.bfloat16), pltpu.VMEM((total, width), jnp.bfloat16)]

    def exchange(matching):
        apart = matching_apart(peers, matching, match_total)
        return lax.ppermute(features, "dom", [(i, i ^ apart) for i in range(peers)])

    ring_of = [(i + 1) % peers if i % 2 else (i - 1) % peers for i in range(peers)]
    far_of = [i ^ matching_apart(peers, 2, match_total) for i in range(peers)]
    swapped = []
    device, end = 0, ring_of[0]
    while end not in swapped:
        ring_of[device], far_of[device] = far_of[device], ring_of[device]
        target = ring_of[device]
        swapped.append(target)
        device = next((i for i in range(peers) if ring_of[i] == target and i != device), None)
    near = matching_apart(peers, 1, match_total)
    core_of, near_of = [i ^ 1 for i in range(peers)], [i ^ near for i in range(peers)]
    for device in (peers - 1, (peers - 1) ^ near ^ 1):
        core_of[device], near_of[device] = near_of[device], core_of[device]
    arrived = {
        "core": lax.ppermute(features, "dom", list(enumerate(core_of))),
        "x": lax.ppermute(features, "dom", list(enumerate(near_of))),
        "y": lax.ppermute(features, "dom", list(enumerate(far_of))),
        "z": exchange(3),
        "ring": lax.ppermute(features, "dom", list(enumerate(ring_of))),
    }
    swapped = tuple(swapped)

    def in_order(kinds, after):
        gathered = []
        for kind in kinds:
            one, after = lax.optimization_barrier((arrived[kind], after))
            gathered.append(one)
        return gathered, after

    far_blocks, far_count = jnp.transpose(expander_blocks, (1, 2, 0)), jnp.transpose(expander_count)
    state = (array(rows, width, dtype=jnp.float32),) * 3
    tables = (local_blocks, local_count, far_blocks, far_count)
    inputs = (features, w_query, w_key, w_value, w_out, *tables)
    near, _ = in_order(FIRST[1:], features)
    x, w_key, w_value, w_out, queries, bias, times, *states = pl.pallas_call(
        first_kernel,
        out_shape=(
            array(rows, width), *[array(width, width)] * 3, array(rows, width),
            array(match_total + 2, groups, rows, dtype=jnp.float32), array(2, groups, rows, dtype=jnp.float32),
            *state,
        ),
        in_specs=[ANY] * len(inputs) + [VMEM] * len(near),
        out_specs=(VMEM,) * 10,
        scratch_shapes=[
            pltpu.VMEM((width, width), jnp.bfloat16),
            *pairs_of(len(FIRST) * rows),
            *(pltpu.SMEM(t.shape, jnp.int32) for t in tables),
            pltpu.SemaphoreType.DMA((len(inputs),)),
        ],
        compiler_params=params,
        name="first",
    )(*(pltpu.with_memory_space_constraint(a, pltpu.HBM) for a in inputs), *near)
    for kinds in MIDDLE:
        near, states = in_order(kinds, states)
        states = pl.pallas_call(
            functools.partial(middle_kernel, kinds, swapped),
            out_shape=state,
            in_specs=[VMEM] * (len(near) + 8),
            out_specs=(VMEM,) * 3,
            scratch_shapes=pairs_of(len(kinds) * rows),
            compiler_params=params,
            name="_".join(kinds),
        )(*near, w_key, w_value, queries, bias, times, *states)
    near, states = in_order(LAST, states)
    return pl.pallas_call(
        last_kernel,
        out_shape=array(rows, width, dtype=features.dtype),
        in_specs=[VMEM] * (len(near) + 10),
        out_specs=VMEM,
        scratch_shapes=pairs_of(len(LAST) * rows),
        compiler_params=params,
        name="last",
    )(*near, w_key, w_value, queries, bias, times, *states, x, w_out)


def solution(mesh):
    in_specs = (
        P("dom", None),
        P(),
        P(),
        P(),
        P(),
        P("dom", None),
        P("dom"),
        P(None, "dom", None),
        P(None, "dom"),
    )
    out_specs = P("dom", None)
    return jax.shard_map(shards, mesh=mesh, in_specs=in_specs, out_specs=out_specs, check_vma=False)
```
